128 devices in a mesh: slab: 64 (over x, z_lo, y, core), patch: 2 (over z_hi).
Axes of the slice: x: 4, y: 4, z: 4 (z_hi: 2, z_lo: 2; z = z_hi * 2 + z_lo), core: 2. Of those that a mesh axis runs over, the one named last changes fastest.
Arguments:
- coarse_phi: float32 [1024, 128, 128], P(('slab', 'patch')), may hold values from -6 to 6
- coarse_rho: float32 [1024, 128, 128], P(('slab', 'patch')), may hold values from -6 to 6
- fine_patch_potential: float32 [256, 64, 4096], P(('slab', 'patch')), may hold values from -6 to 6
- fine_patch_source: float32 [256, 64, 4096], P(('slab', 'patch')), may hold values from -96 to 96
- anchors: int32 [256, 2], P('slab'), may hold values from 1 to 111
- owned_count: int32 [128], P('slab'), may hold values from 0 to 2, as said below
- colour_order: int32 [4], replicated, may hold values from 0 to 1
Outputs:
- coarse_out: float32 [1024, 128, 128], P(('slab', 'patch'))
- patch_out: float32 [256, 64, 4096], P(('slab', 'patch'))
The draws below stay inside these ranges and needn't reach their ends.
Inputs may be any that keep to these rules, and one draw needn't show every extreme that they name: A device's live patches are its first owned_count slots; the two devices of one slab group (indices 2 g and 2 g + 1) hold at most 2 live patches together, and some group holds exactly 2. `anchors`: every region and the layer of cells around it lie inside the grid in x and y.
All inputs are finite; a program needn't handle non-finite values.
Results may differ from the reference program's by a relative error of at most 0.0003.
Values sent between devices are 32-bit elements; how exact they have to be, the bound alone decides.
A program may use at most 192 MiB of HBM per device.

```python
import jax
import jax.numpy as jnp
from jax import lax

COARSE_PLANE = 128
LOCAL_SLOTS = 2
PATCH_FINE = 64
RATIO = 4
SWEEPS = 4
PATCH_COARSE = 16
CZ = 8
NZ = 1024
TOTAL_SLOTS = 256


def draw_owned_count(key, part):
    slot_groups = TOTAL_SLOTS // LOCAL_SLOTS // 2
    key_total, key_leading, key_group, key_owner = jax.random.split(key, 4)
    totals = LOCAL_SLOTS - jax.random.randint(key_total, (slot_groups,), 0, 2)
    leading = jax.random.randint(key_leading, (slot_groups,), 0, totals + 1)
    chosen = jax.random.randint(key_group, (), 0, slot_groups)
    owner_side = jax.random.randint(key_owner, (), 0, 2)
    positions = jnp.arange(slot_groups)
    leading = jnp.where(positions == chosen, owner_side * LOCAL_SLOTS, leading)
    totals = jnp.where(positions == chosen, LOCAL_SLOTS, totals)
    trailing = totals - leading
    return jnp.stack([leading, trailing], axis=1).reshape(slot_groups * 2).astype(jnp.int32)


def set_ends(entries, rng, smallest, high):
    longest = entries.shape.index(max(entries.shape))
    spots = []
    for shift in (0, 1):
        where = [jax.random.randint(jax.random.fold_in(rng, axis), (), 0, length) for axis, length in enumerate(entries.shape)]
        where[longest] = (where[longest] + shift) % entries.shape[longest]
        spots.append(tuple(where))
    return entries.at[spots[0]].set(smallest).at[spots[1]].set(high)


def level_of(stream_key, shape, cuts, low, top_value):
    level, own = 1.0, jax.random.fold_in(stream_key, 6)
    for position, shards_of in cuts:
        steps = jnp.exp(jax.random.uniform(jax.random.fold_in(own, position), (shards_of,), jnp.float32, low / len(cuts), top_value / len(cuts)))
        level = level * jnp.repeat(steps, shape[position] // shards_of).reshape([-1 if axis == position else 1 for axis in range(len(shape))])
    return level


def bell_draw(key, shape, scale, bound, cuts=(), held_as=jnp.bfloat16):
    entries = scale * jax.random.normal(key, shape, jnp.float32)
    if cuts:
        entries = entries * level_of(key, shape, cuts, -0.22, 0.18)
    return jnp.clip(entries, -bound, bound).astype(held_as)


def setup_inputs(seed: int = 0) -> dict:
    splits = jax.random.split(jax.random.key(seed), 8)
    return {
        "coarse_phi": bell_draw(splits[0], (NZ, COARSE_PLANE, COARSE_PLANE), 1.0, 6.0, ((0, 128),), jnp.float32),
        "coarse_rho": bell_draw(splits[1], (NZ, COARSE_PLANE, COARSE_PLANE), 1.0, 6.0, ((0, 128),), jnp.float32),
        "fine_patch_potential": bell_draw(splits[2], (TOTAL_SLOTS, PATCH_FINE, PATCH_FINE * PATCH_FINE), 1.0, 6.0, ((0, 128),), jnp.float32),
        "fine_patch_source": bell_draw(splits[3], (TOTAL_SLOTS, PATCH_FINE, PATCH_FINE * PATCH_FINE), 16.0, 96.0, ((0, 128),), jnp.float32),
        "anchors": set_ends(jax.random.randint(splits[4], (TOTAL_SLOTS, 2), 1, COARSE_PLANE - PATCH_COARSE), jax.random.fold_in(splits[4], 1), 1, (COARSE_PLANE - PATCH_COARSE) - 1).astype(jnp.int32),
        "owned_count": draw_owned_count(jax.random.fold_in(splits[7], 71), 0),
        "colour_order": set_ends(jax.random.randint(splits[6], (SWEEPS,), 0, 2), jax.random.fold_in(splits[6], 1), 0, 1).astype(jnp.int32),
    }


accel_scale = 1.0


def int_starts(*values):
    return tuple(jnp.asarray(value).astype(jnp.int32) for value in values)


def face_weight(near_value, center, inverse_step):
    return 1.0 + 1.0 / (1.0 + inverse_step * jnp.abs(near_value - center) / accel_scale)


def relax(center, neighbours, source, inverse_step, step_square, update):
    weight_sum = jnp.zeros_like(center)
    weighted = jnp.zeros_like(center)
    for near_value in neighbours:
        weight = face_weight(near_value, center, inverse_step)
        weight_sum = weight_sum + weight
        weighted = weighted + weight * near_value
    relaxed = (weighted - step_square * source) / weight_sum
    return jnp.where(update, relaxed, center)


def coarse_colour(coarse_field, coarse_rho, colour):
    padded = jnp.pad(coarse_field, 1)
    across = jnp.arange(COARSE_PLANE, dtype=jnp.int32)
    plane_sum = across[:, None] + across[None, :]

    def one_block(block_index):
        z_begin = block_index * CZ
        window = lax.dynamic_slice(padded, int_starts(z_begin, 0, 0), (CZ + 2, COARSE_PLANE + 2, COARSE_PLANE + 2))
        source_block = lax.dynamic_slice(coarse_rho, int_starts(z_begin, 0, 0), (CZ, COARSE_PLANE, COARSE_PLANE))
        z_values = z_begin + jnp.arange(CZ, dtype=jnp.int32)
        update = ((z_values[:, None, None] + plane_sum[None]) % 2) == colour
        center = window[1:-1, 1:-1, 1:-1]
        neighbours = [window[:-2, 1:-1, 1:-1], window[2:, 1:-1, 1:-1], window[1:-1, :-2, 1:-1],
                      window[1:-1, 2:, 1:-1], window[1:-1, 1:-1, :-2], window[1:-1, 1:-1, 2:]]
        return relax(center, neighbours, source_block, 1.0, 1.0, update)

    blocks = lax.map(one_block, jnp.arange(NZ // CZ, dtype=jnp.int32))
    return blocks.reshape(NZ, COARSE_PLANE, COARSE_PLANE)


def all_shells(coarse_field, anchors):
    padded = jnp.pad(coarse_field, 1)

    def single_cut(slot_id, anchor):
        z_start = ((slot_id // LOCAL_SLOTS) // 2) * PATCH_COARSE
        x_anchor = anchor[0]
        y_anchor = anchor[1]
        x_low = lax.dynamic_slice(padded, int_starts(z_start + 1, y_anchor + 1, x_anchor), (PATCH_COARSE, PATCH_COARSE, 1)).reshape(PATCH_COARSE, PATCH_COARSE)
        x_high = lax.dynamic_slice(padded, int_starts(z_start + 1, y_anchor + 1, x_anchor + PATCH_COARSE + 1), (PATCH_COARSE, PATCH_COARSE, 1)).reshape(PATCH_COARSE, PATCH_COARSE)
        y_low = lax.dynamic_slice(padded, int_starts(z_start + 1, y_anchor, x_anchor + 1), (PATCH_COARSE, 1, PATCH_COARSE)).reshape(PATCH_COARSE, PATCH_COARSE)
        y_high = lax.dynamic_slice(padded, int_starts(z_start + 1, y_anchor + PATCH_COARSE + 1, x_anchor + 1), (PATCH_COARSE, 1, PATCH_COARSE)).reshape(PATCH_COARSE, PATCH_COARSE)
        under = lax.dynamic_slice(padded, int_starts(z_start, y_anchor + 1, x_anchor + 1), (1, PATCH_COARSE, PATCH_COARSE)).reshape(PATCH_COARSE, PATCH_COARSE)
        above = lax.dynamic_slice(padded, int_starts(z_start + PATCH_COARSE + 1, y_anchor + 1, x_anchor + 1), (1, PATCH_COARSE, PATCH_COARSE)).reshape(PATCH_COARSE, PATCH_COARSE)
        return jnp.stack([x_low, x_high, y_low, y_high, under, above])

    return jax.vmap(single_cut)(jnp.arange(TOTAL_SLOTS, dtype=jnp.int32), anchors)


def expand(face):
    return jnp.repeat(jnp.repeat(face, RATIO, axis=0), RATIO, axis=1)


def fine_sweeps(potential, density, shell_set, is_live, colour_order):
    fine_field = potential.reshape(PATCH_FINE, PATCH_FINE, PATCH_FINE)
    dense_cube = density.reshape(PATCH_FINE, PATCH_FINE, PATCH_FINE)
    grid = jnp.arange(PATCH_FINE, dtype=jnp.int32)
    fine_parity = (grid[:, None, None] + grid[None, :, None] + grid[None, None, :]) % 2
    for sweep_index in range(SWEEPS):
        face_set = shell_set[sweep_index]
        frame = jnp.zeros((PATCH_FINE + 2, PATCH_FINE + 2, PATCH_FINE + 2), jnp.float32)
        frame = frame.at[1:-1, 1:-1, 0].set(expand(face_set[0]))
        frame = frame.at[1:-1, 1:-1, -1].set(expand(face_set[1]))
        frame = frame.at[1:-1, 0, 1:-1].set(expand(face_set[2]))
        frame = frame.at[1:-1, -1, 1:-1].set(expand(face_set[3]))
        frame = frame.at[0, 1:-1, 1:-1].set(expand(face_set[4]))
        frame = frame.at[-1, 1:-1, 1:-1].set(expand(face_set[5]))
        first_colour = colour_order[sweep_index]
        for colour in (first_colour, 1 - first_colour):
            frame = frame.at[1:-1, 1:-1, 1:-1].set(fine_field)
            neighbours = [frame[:-2, 1:-1, 1:-1], frame[2:, 1:-1, 1:-1], frame[1:-1, :-2, 1:-1],
                          frame[1:-1, 2:, 1:-1], frame[1:-1, 1:-1, :-2], frame[1:-1, 1:-1, 2:]]
            fine_field = relax(fine_field, neighbours, dense_cube, float(RATIO), 1.0 / (RATIO * RATIO),
                               fine_parity == colour)
    return jnp.where(is_live, fine_field.reshape(PATCH_FINE, PATCH_FINE * PATCH_FINE), potential)


def reference(coarse_phi, coarse_rho, fine_patch_potential, fine_patch_source, anchors, owned_count, colour_order):
    coarse_field = coarse_phi
    shell_list = []
    for sweep_index in range(SWEEPS):
        shell_list.append(all_shells(coarse_field, anchors))
        first_colour = colour_order[sweep_index]
        coarse_field = coarse_colour(coarse_field, coarse_rho, first_colour)
        coarse_field = coarse_colour(coarse_field, coarse_rho, 1 - first_colour)
    shells = jnp.stack(shell_list, axis=1)
    slot_numbers = jnp.arange(TOTAL_SLOTS, dtype=jnp.int32)
    is_live = (slot_numbers % LOCAL_SLOTS) < owned_count[slot_numbers // LOCAL_SLOTS]
    patch_out = lax.map(lambda members: fine_sweeps(members[0], members[1], members[2], members[3], colour_order),
                        (fine_patch_potential, fine_patch_source, shells, is_live))
    return coarse_field, patch_out
```

```python
import functools

import jax
import jax.numpy as jnp
from jax import lax
from jax.experimental import pallas as pl
from jax.experimental.pallas import tpu as pltpu
from jax.sharding import PartitionSpec as P

MESH = pl.DeviceIdType.MESH
SWEEPS = 4
N = 128
CZ = 8
PAIRS = CZ // 2
SLOTS = 2
FINE = 64
HALF = FINE // 2
WIN = 16
TOP = 8
FULL = N + 8
JB = 8


def relaxed(center, neighbours, source):
    r_sum = rv_sum = v_sum = None
    for value in neighbours:
        r = pl.reciprocal(1.0 + jnp.abs(value - center), approx=True)
        rv = r * value
        r_sum = r if r_sum is None else r_sum + r
        rv_sum = rv if rv_sum is None else rv_sum + rv
        v_sum = value if v_sum is None else v_sum + value
    return (rv_sum + (v_sum - source)) * pl.reciprocal(6.0 + r_sum, approx=True)


def iota(shape, dim):
    return lax.broadcasted_iota(jnp.int32, shape, dim)


def split_dot(rows, onehot):
    high = rows.astype(jnp.bfloat16)
    low = (rows - high.astype(jnp.float32)).astype(jnp.bfloat16)
    return jnp.dot(high, onehot, preferred_element_type=jnp.float32) + jnp.dot(
        low, onehot, preferred_element_type=jnp.float32
    )


def kernel(
    groups,
    anchors, owned, order, phi_hbm, rho_hbm, pot_hbm, src_hbm,
    coarse_hbm, patch_hbm,
    raw_phi, raw_rho, raw_pot, raw_src,
    ca, cb, rho_c, halo_rx, rho_rx, full, w_own, w_send, w_rx, far_rx, zplanes, w_rows,
    pa, pb, src_c, x_face, sx, ey, out_stage,
    in_sem, out_sem, halo_send, halo_recv, rho_send, rho_recv, w_ssem, w_rsem, far_send, far_recv,
):
    g = lax.axis_index("slab")
    p = lax.axis_index("patch")
    has_up = jnp.logical_or(g < groups - 1, p == 0)
    has_dn = jnp.logical_or(g > 0, p == 1)
    far_to_ok = jnp.where(p == 0, g > 0, g < groups - 1)
    far_from_ok = jnp.where(p == 0, g < groups - 1, g > 0)
    wrap = lambda v: lax.rem(v + groups, groups)
    up = (wrap(g + p), 1 - p)
    dn = (wrap(g - 1 + p), 1 - p)
    partner = (g, 1 - p)
    far_to = (wrap(g + 2 * p - 1), p)
    far_from = (wrap(g + 1 - 2 * p), p)

    loads = [
        pltpu.make_async_copy(phi_hbm, raw_phi, in_sem.at[0]),
        pltpu.make_async_copy(rho_hbm, raw_rho, in_sem.at[1]),
    ]
    for load in loads:
        load.start()

    def columns(j):
        return pl.ds(pl.multiple_of(j * N, N), N)

    barrier = pltpu.get_barrier_semaphore()
    greeted = ((up, has_up), (dn, has_dn), (far_to, far_to_ok), (far_from, far_from_ok))
    for device, ok in greeted:
        @pl.when(ok)
        def _(device=device):
            pl.semaphore_signal(barrier, inc=1, device_id=device, device_id_type=MESH)

    def fetch(j, carry):
        for slot in range(SLOTS):
            pltpu.make_async_copy(pot_hbm.at[slot, :, columns(j)], raw_pot.at[slot, j], in_sem.at[2]).start()
            pltpu.make_async_copy(src_hbm.at[slot, :, columns(j)], raw_src.at[slot, j], in_sem.at[3]).start()
        return carry

    lax.fori_loop(0, HALF, fetch, 0)

    rows = pl.ds(TOP, N)
    bufs = (ca, cb)

    def halo_copy(s, b, role, side):
        return pltpu.make_async_remote_copy(
            src_ref=bufs[b].at[role, 1 if side == 0 else PAIRS, rows],
            dst_ref=halo_rx.at[s, role, 1 - side],
            send_sem=halo_send.at[s, role, side],
            recv_sem=halo_recv.at[s, role, 1 - side],
            device_id=dn if side == 0 else up,
            device_id_type=MESH,
        )

    def rho_copy(side):
        return pltpu.make_async_remote_copy(
            src_ref=raw_rho.at[0 if side == 0 else CZ - 1],
            dst_ref=rho_rx.at[1 - side],
            send_sem=rho_send.at[side],
            recv_sem=rho_recv.at[1 - side],
            device_id=dn if side == 0 else up,
            device_id_type=MESH,
        )

    def w_copy(s):
        return pltpu.make_async_remote_copy(
            src_ref=w_send, dst_ref=w_rx.at[s], send_sem=w_ssem, recv_sem=w_rsem.at[s],
            device_id=partner, device_id_type=MESH,
        )

    def far_copy(s):
        return pltpu.make_async_remote_copy(
            src_ref=full.at[pl.ds(p * ((CZ - 1) * FULL), N)],
            dst_ref=far_rx.at[s],
            send_sem=far_send,
            recv_sem=far_recv.at[s],
            device_id=far_to,
            device_id_type=MESH,
        )

    def send_halo(s, b, role):
        for side, ok in ((0, has_dn), (1, has_up)):
            @pl.when(ok)
            def _(side=side):
                halo_copy(s, b, role, side).start()

    plane_parity = (iota((N, N), 0) + iota((N, N), 1)) % 2
    lane_c = iota((N, N), 1)
    lane_p = iota((HALF, N), 1)
    fine_parity = (lane_p // FINE + lane_p) % 2
    x_first = lane_p % FINE == 0
    x_last = lane_p % FINE == FINE - 1
    y_first = lane_p < FINE

    for buf in bufs:
        for role in range(2):
            for i in range(PAIRS + 2):
                buf[role, i, 0:TOP, :] = jnp.zeros((TOP, N), jnp.float32)
                buf[role, i, TOP + N :, :] = jnp.zeros((TOP, N), jnp.float32)

    loads[0].wait()
    for i in range(PAIRS):
        even, odd = raw_phi[2 * i], raw_phi[2 * i + 1]
        ca[0, i + 1, rows, :] = jnp.where(plane_parity == 0, even, odd)
        ca[1, i + 1, rows, :] = jnp.where(plane_parity == 0, odd, even)

    pl.semaphore_wait(barrier, sum(ok.astype(jnp.int32) for _, ok in greeted))

    send_halo(0, 0, 0)
    send_halo(0, 0, 1)
    loads[1].wait()
    for side, ok in ((0, has_dn), (1, has_up)):
        @pl.when(ok)
        def _(side=side):
            rho_copy(side).start()

    def extract(s, b, role0_colour):
        for i in range(PAIRS):
            first, second = bufs[b][0, i + 1, rows, :], bufs[b][1, i + 1, rows, :]
            here = plane_parity == role0_colour
            full[pl.ds(2 * i * FULL, N), :] = jnp.where(here, first, second)
            full[pl.ds((2 * i + 1) * FULL, N), :] = jnp.where(here, second, first)

        @pl.when(far_to_ok)
        def _():
            far_copy(s).start()

        lane = iota((CZ, N), 1)
        for whose, dst in ((1 - p, w_send), (p, w_own)):
            packed = jnp.zeros((CZ, N), jnp.float32)
            for k in range(SLOTS):
                ox = anchors[0, whose * SLOTS + k]
                oy = jnp.maximum(anchors[1, whose * SLOTS + k], 1)
                base = k * FINE
                for t in range(WIN):
                    line = full[pl.ds(oy + t, CZ, stride=FULL), :]
                    low = pltpu.roll(line, lax.rem(base + t - (ox - 1) + 2 * N, N), 1)
                    high = pltpu.roll(line, lax.rem(base + WIN + t - (ox + WIN) + 2 * N, N), 1)
                    packed = jnp.where(lane == base + t, low, packed)
                    packed = jnp.where(lane == base + WIN + t, high, packed)
                for kind, row in ((2, oy - 1), (3, oy + WIN)):
                    line = full[pl.ds(row, CZ, stride=FULL), :]
                    line = pltpu.roll(line, lax.rem(base + kind * WIN - ox + 2 * N, N), 1)
                    inside = jnp.logical_and(lane >= base + kind * WIN, lane < base + (kind + 1) * WIN)
                    packed = jnp.where(inside, line, packed)
            dst[...] = packed
        w_copy(s).start()

    extract(0, 0, 0)
    for i in range(PAIRS):
        even, odd = raw_rho[2 * i], raw_rho[2 * i + 1]
        rho_c[0, i + 1] = jnp.where(plane_parity == 0, even, odd)
        rho_c[1, i + 1] = jnp.where(plane_parity == 0, odd, even)

    pltpu.make_async_copy(raw_pot, raw_pot, in_sem.at[2]).wait()
    pltpu.make_async_copy(raw_src, raw_src, in_sem.at[3]).wait()
    for slot in range(SLOTS):
        def split(j, carry, slot=slot):
            for raw, scale, put in ((raw_pot, 4.0, 0), (raw_src, 0.25, 1)):
                even = scale * raw[slot, j, pl.ds(0, HALF, stride=2), :]
                odd = scale * raw[slot, j, pl.ds(1, HALF, stride=2), :]
                zero = jnp.where(fine_parity == 0, even, odd)
                one = jnp.where(fine_parity == 0, odd, even)
                if put == 0:
                    pa[slot, 0, j + 1, pl.ds(TOP, HALF), :] = zero
                    pa[slot, 1, j + 1, pl.ds(TOP, HALF), :] = one
                else:
                    src_c[slot, 0, j] = zero
                    src_c[slot, 1, j] = one
            return carry

        lax.fori_loop(0, HALF, split, 0)
        ox = anchors[0, p * SLOTS + slot]
        row, lane = iota((N, N), 0), lane_c
        sx[slot] = (row == ox + (lane % FINE) // 4).astype(jnp.float32).astype(jnp.bfloat16)
        wanted = slot * FINE + jnp.where(lane < FINE, 3 * WIN, 2 * WIN) + (lane % FINE) // 4
        ey[slot] = (row == wanted).astype(jnp.float32).astype(jnp.bfloat16)

    def coarse_pairs(b, role_c, role_b, role_out, q, pairs, first_half):
        cur, nxt = bufs[b], bufs[1 - b]
        other = cur if first_half else nxt
        outs = []
        for i in pairs:
            center = cur[role_c, i, rows, :]
            near = other[role_b, i, rows, :]
            below = other[role_b, max(i - 1, 0), rows, :]
            above = other[role_b, min(i + 1, PAIRS + 1), rows, :]
            outs.append(
                relaxed(
                    center,
                    (
                        near,
                        jnp.where(plane_parity == q, below, above),
                        other[role_b, i, pl.ds(TOP - 1, N), :],
                        other[role_b, i, pl.ds(TOP + 1, N), :],
                        jnp.where(lane_c == 0, 0.0, pltpu.roll(near, 1, 1)),
                        jnp.where(lane_c == N - 1, 0.0, pltpu.roll(near, N - 1, 1)),
                    ),
                    rho_c[q, i],
                )
            )
        for i, out in zip(pairs, outs):
            nxt[role_out, i, rows, :] = out

    def patch_half(slot, center_ref, role_c, other_ref, role_b, out_ref, role_out, q):
        data = pl.ds(TOP, HALF)

        def step(k, carry):
            j0 = k * JB
            b = [other_ref[slot, role_b, j0 + t, data, :] for t in range(JB + 2)]
            across = [pltpu.roll(jnp.where(y_first, b[t + 1], b[t]), FINE, 1) for t in range(JB + 1)]
            outs = []
            for t in range(JB):
                below = other_ref[slot, role_b, j0 + t + 1, pl.ds(TOP - 1, HALF), :]
                above = other_ref[slot, role_b, j0 + t + 1, pl.ds(TOP + 1, HALF), :]
                face = x_face[k * (JB // 2) + t // 2]
                near = b[t + 1]
                outs.append(
                    relaxed(
                        center_ref[slot, role_c, j0 + t + 1, data, :],
                        (
                            near,
                            jnp.where(fine_parity == q, below, above),
                            across[t],
                            across[t + 1],
                            jnp.where(x_first, face, pltpu.roll(near, 1, 1)),
                            jnp.where(x_last, face, pltpu.roll(near, N - 1, 1)),
                        ),
                        src_c[slot, q, j0 + t],
                    )
                )
            for t in range(JB):
                out_ref[slot, role_out, j0 + t + 1, data, :] = outs[t]
            return carry

        lax.fori_loop(0, HALF // JB, step, 0)

    def faces_of(slot, prev, nxt):
        data = pl.ds(TOP, HALF)
        w = 4.0 * w_rows[...]
        for t in range(WIN):
            low = jnp.broadcast_to(w[:, slot * FINE + t : slot * FINE + t + 1], (HALF, N))
            high = jnp.broadcast_to(w[:, slot * FINE + WIN + t : slot * FINE + WIN + t + 1], (HALF, N))
            x_face[t] = jnp.where(x_last, high, low)
        y_face = split_dot(w, ey[slot])
        oy = jnp.maximum(anchors[1, p * SLOTS + slot], 1)
        z_rows = jnp.concatenate([zplanes[0, pl.ds(oy, WIN), :], zplanes[1, pl.ds(oy, WIN), :]], axis=0)
        z_face = split_dot(4.0 * z_rows, sx[slot])
        for ref, role in ((prev, 0), (prev, 1), (nxt, 0)):
            ref[slot, role, 0, data, :] = y_face
            ref[slot, role, HALF + 1, data, :] = y_face
            for j in range(HALF):
                ref[slot, role, j + 1, TOP - 1 : TOP, :] = z_face[j // 2 : j // 2 + 1]
                ref[slot, role, j + 1, TOP + HALF : TOP + HALF + 1, :] = z_face[WIN + j // 2 : WIN + j // 2 + 1]

    patch_bufs = (pa, pb)

    def sweep(s, b, last):
        q = order[s]
        before = order[jnp.maximum(s - 1, 0)]
        first = jnp.where(s == 0, q, jnp.where(q == before, 0, 1))
        role0_colour = jnp.where(s == 0, 0, before)
        cur, nxt = bufs[b], bufs[1 - b]

        for side, ok, i in ((0, has_dn, 0), (1, has_up, PAIRS + 1)):
            @pl.when(ok)
            def _(side=side, i=i):
                for role in range(2):
                    halo_copy(s, b, role, 1 - side).wait_recv()
                    cur[role, i, rows, :] = halo_rx[s, role, side]

                @pl.when(s == 0)
                def _():
                    rho_copy(1 - side).wait_recv()
                    plane = rho_rx[side]
                    rho_c[0, i] = plane
                    rho_c[1, i] = plane

            @pl.when(jnp.logical_not(ok))
            def _(side=side, i=i):
                for role in range(2):
                    cur[role, i, rows, :] = jnp.zeros((N, N), jnp.float32)
                    rho_c[role, i] = jnp.zeros((N, N), jnp.float32)

        near_first, near_second = cur[0, p * (PAIRS + 1), rows, :], cur[1, p * (PAIRS + 1), rows, :]
        zplanes[p] = jnp.where(plane_parity == (role0_colour + 1 - p) % 2, near_first, near_second)

        def settle():
            for side, ok in ((0, has_dn), (1, has_up)):
                @pl.when(ok)
                def _(side=side):
                    for role in range(2):
                        halo_copy(s, b, role, side).wait_send()

                    @pl.when(s == 0)
                    def _():
                        rho_copy(side).wait_send()

            @pl.when(far_to_ok)
            def _():
                far_copy(s).wait_send()

            w_copy(s).wait_send()

        def send_next(role):
            if not last:
                send_halo(s + 1, 1 - b, role)
            else:
                @pl.when(s < SWEEPS - 1)
                def _():
                    send_halo(s + 1, 1 - b, role)

        coarse_pairs(b, first, 1 - first, 0, q, (1, PAIRS), True)
        send_next(0)
        coarse_pairs(b, first, 1 - first, 0, q, (0, 2), True)
        coarse_pairs(b, first, 1 - first, 0, q, (PAIRS - 1, PAIRS + 1), True)
        for ok, i in ((has_dn, 0), (has_up, PAIRS + 1)):
            @pl.when(jnp.logical_not(ok))
            def _(i=i):
                nxt[0, i, rows, :] = jnp.zeros((N, N), jnp.float32)
        coarse_pairs(b, 1 - first, 0, 1, 1 - q, (1, PAIRS), False)
        send_next(1)
        coarse_pairs(b, 1 - first, 0, 1, 1 - q, (2, PAIRS - 1), False)

        w_copy(s).wait_recv()
        mine, theirs = w_own[...], w_rx[s]
        lower = jnp.where(p == 0, mine, theirs)
        upper = jnp.where(p == 0, theirs, mine)
        for t in range(2):
            w_rows[pl.ds(t, CZ, stride=2), :] = lower
            w_rows[pl.ds(2 * CZ + t, CZ, stride=2), :] = upper

        @pl.when(far_from_ok)
        def _():
            far_copy(s).wait_recv()
            zplanes[1 - p] = far_rx[s]

        @pl.when(jnp.logical_not(far_from_ok))
        def _():
            zplanes[1 - p] = jnp.zeros((N, N), jnp.float32)

        settle()
        if not last:
            extract(s + 1, 1 - b, q)
        else:
            @pl.when(s < SWEEPS - 1)
            def _():
                extract(s + 1, 1 - b, q)

            @pl.when(s == SWEEPS - 1)
            def _():
                for i in range(PAIRS):
                    one, two = nxt[0, i + 1, rows, :], nxt[1, i + 1, rows, :]
                    raw_phi[2 * i] = jnp.where(plane_parity == q, one, two)
                    raw_phi[2 * i + 1] = jnp.where(plane_parity == q, two, one)
                pltpu.make_async_copy(raw_phi, coarse_hbm, out_sem.at[SLOTS]).start()

        for slot in range(SLOTS):
            now, new = patch_bufs[b], patch_bufs[1 - b]
            faces_of(slot, now, new)
            patch_half(slot, now, first, now, 1 - first, new, 0, q)
            patch_half(slot, now, 1 - first, new, 0, new, 1, 1 - q)
            if last:
                @pl.when(s == SWEEPS - 1)
                def _(slot=slot, new=new):
                    live = slot < owned[p]

                    def join(j, carry):
                        one = 0.25 * new[slot, 0, j + 1, pl.ds(TOP, HALF), :]
                        two = 0.25 * new[slot, 1, j + 1, pl.ds(TOP, HALF), :]
                        for odd in range(2):
                            z = pl.ds(odd, HALF, stride=2)
                            swept = jnp.where(fine_parity == (q + odd) % 2, one, two)
                            out_stage[slot, j, z, :] = jnp.where(live, swept, raw_pot[slot, j, z, :])
                        pltpu.make_async_copy(
                            out_stage.at[slot, j], patch_hbm.at[slot, :, columns(j)], out_sem.at[slot]
                        ).start()
                        return carry

                    lax.fori_loop(0, HALF, join, 0)

    def two_sweeps(t, carry):
        sweep(2 * t, 0, False)
        sweep(2 * t + 1, 1, True)
        return carry

    lax.fori_loop(0, SWEEPS // 2, two_sweeps, 0)
    pltpu.make_async_copy(raw_phi, coarse_hbm, out_sem.at[SLOTS]).wait()
    for slot in range(SLOTS):
        pltpu.make_async_copy(out_stage.at[slot], out_stage.at[slot], out_sem.at[slot]).wait()


def on_device(groups, phi, rho, pot, src, anchors, owned, order):
    f32, bf16 = jnp.float32, jnp.bfloat16
    dma = pltpu.SemaphoreType.DMA
    smem = pl.BlockSpec(memory_space=pltpu.SMEM)
    hbm = pl.BlockSpec(memory_space=pl.ANY)
    return pl.pallas_call(
        functools.partial(kernel, groups),
        out_shape=(jax.ShapeDtypeStruct(phi.shape, f32), jax.ShapeDtypeStruct(pot.shape, f32)),
        in_specs=[smem] * 3 + [hbm] * 4,
        out_specs=(hbm, hbm),
        scratch_shapes=[
            pltpu.VMEM((CZ, N, N), f32),
            pltpu.VMEM((CZ, N, N), f32),
            pltpu.VMEM((SLOTS, HALF, FINE, N), f32),
            pltpu.VMEM((SLOTS, HALF, FINE, N), f32),
            pltpu.VMEM((2, PAIRS + 2, N + 2 * TOP, N), f32),
            pltpu.VMEM((2, PAIRS + 2, N + 2 * TOP, N), f32),
            pltpu.VMEM((2, PAIRS + 2, N, N), f32),
            pltpu.VMEM((SWEEPS, 2, 2, N, N), f32),
            pltpu.VMEM((2, N, N), f32),
            pltpu.VMEM((CZ * FULL, N), f32),
            pltpu.VMEM((CZ, N), f32),
            pltpu.VMEM((CZ, N), f32),
            pltpu.VMEM((SWEEPS, CZ, N), f32),
            pltpu.VMEM((SWEEPS, N, N), f32),
            pltpu.VMEM((2, N, N), f32),
            pltpu.VMEM((HALF, N), f32),
            pltpu.VMEM((SLOTS, 2, HALF + 2, HALF + 2 * TOP, N), f32),
            pltpu.VMEM((SLOTS, 2, HALF + 2, HALF + 2 * TOP, N), f32),
            pltpu.VMEM((SLOTS, 2, HALF, HALF, N), f32),
            pltpu.VMEM((WIN, HALF, N), f32),
            pltpu.VMEM((SLOTS, N, N), bf16),
            pltpu.VMEM((SLOTS, N, N), bf16),
            pltpu.VMEM((SLOTS, HALF, FINE, N), f32),
            dma((4,)),
            dma((SLOTS + 1,)),
            dma((SWEEPS, 2, 2)),
            dma((SWEEPS, 2, 2)),
            dma((2,)),
            dma((2,)),
            dma,
            dma((SWEEPS,)),
            dma,
            dma((SWEEPS,)),
        ],
        compiler_params=pltpu.CompilerParams(
            collective_id=0, has_side_effects=True, vmem_limit_bytes=62 << 20
        ),
        name="smooth",
    )(anchors.T, owned, order, phi, rho, pot, src)


def solution(mesh):
    in_specs = (
        P(("slab", "patch"), None, None),
        P(("slab", "patch"), None, None),
        P(("slab", "patch"), None, None),
        P(("slab", "patch"), None, None),
        P("slab", None),
        P("slab"),
        P(),
    )
    out_specs = (P(("slab", "patch"), None, None), P(("slab", "patch"), None, None))
    return jax.shard_map(
        functools.partial(on_device, mesh.shape["slab"]),
        mesh=mesh, in_specs=in_specs, out_specs=out_specs, check_vma=False,
    )
```

```python
import functools

import jax
import jax.numpy as jnp
from jax import lax
from jax.experimental import pallas as pl
from jax.experimental.pallas import tpu as pltpu
from jax.sharding import PartitionSpec as P

MESH = pl.DeviceIdType.MESH
SWEEPS = 4
N = 128
CZ = 8
PAIRS = CZ // 2
SLOTS = 2
FINE = 64
HALF = FINE // 2
WIN = 16
TOP = 8
FULL = N + 8
JB = 8


def relaxed(center, neighbours, source):
    r_sum = rv_sum = v_sum = None
    for value in neighbours:
        r = pl.reciprocal(1.0 + jnp.abs(value - center), approx=True)
        rv = r * value
        r_sum = r if r_sum is None else r_sum + r
        rv_sum = rv if rv_sum is None else rv_sum + rv
        v_sum = value if v_sum is None else v_sum + value
    return (rv_sum + (v_sum - source)) * pl.reciprocal(6.0 + r_sum, approx=True)


def iota(shape, dim):
    return lax.broadcasted_iota(jnp.int32, shape, dim)


def split_dot(rows, onehot):
    high = rows.astype(jnp.bfloat16)
    low = (rows - high.astype(jnp.float32)).astype(jnp.bfloat16)
    return jnp.dot(high, onehot, preferred_element_type=jnp.float32) + jnp.dot(
        low, onehot, preferred_element_type=jnp.float32
    )


def kernel(
    groups,
    anchors, owned, order, phi_hbm, rho_hbm, pot_hbm, src_hbm,
    coarse_hbm, patch_hbm,
    full, raw_rho, raw_pot, raw_src,
    ca, cb, halo, rho_c, rho_h, near_rx, half_send, half_rx, rho_send, rho_rx,
    w_own, w_send, w_rx, far_rx, zplanes, w_rows, pa, pb, src_c, x_face, sx, ey, coarse_stage, out_stage,
    in_sem, out_sem, near_ssem, near_rsem, half_ssem, half_rsem, rho_ssem, rho_rsem,
    w_ssem, w_rsem, far_ssem, far_rsem,
):
    g = lax.axis_index("slab")
    p = lax.axis_index("patch")
    has_up = jnp.logical_or(g < groups - 1, p == 0)
    has_dn = jnp.logical_or(g > 0, p == 1)
    far_to_ok = jnp.where(p == 0, g > 0, g < groups - 1)
    far_from_ok = jnp.where(p == 0, g < groups - 1, g > 0)
    wrap = lambda v: lax.rem(v + groups, groups)
    up = (wrap(g + p), 1 - p)
    dn = (wrap(g - 1 + p), 1 - p)
    partner = (g, 1 - p)
    far_to = (wrap(g + 2 * p - 1), p)
    far_from = (wrap(g + 1 - 2 * p), p)
    sides = ((0, has_dn), (1, has_up))

    barrier = pltpu.get_barrier_semaphore()
    greeted = ((up, has_up), (dn, has_dn), (far_to, far_to_ok), (far_from, far_from_ok))
    for device, ok in greeted:
        @pl.when(ok)
        def _(device=device):
            pl.semaphore_signal(barrier, inc=1, device_id=device, device_id_type=MESH)

    def plane(z):
        return pl.ds(z * FULL, N)

    loads = [pltpu.make_async_copy(phi_hbm.at[z], full.at[plane(z)], in_sem.at[z]) for z in range(CZ)]
    loads.append(pltpu.make_async_copy(rho_hbm, raw_rho, in_sem.at[CZ]))
    for load in loads:
        load.start()

    def columns(j):
        return pl.ds(pl.multiple_of(j * N, N), N)

    def fetch(j, carry):
        for slot in range(SLOTS):
            pltpu.make_async_copy(
                pot_hbm.at[slot, :, columns(j)], raw_pot.at[slot, j], in_sem.at[CZ + 1]
            ).start()
            pltpu.make_async_copy(
                src_hbm.at[slot, :, columns(j)], raw_src.at[slot, j], in_sem.at[CZ + 2]
            ).start()
        return carry

    rows = pl.ds(TOP, N)
    bufs = (ca, cb)

    def near_copy(s, side):
        return pltpu.make_async_remote_copy(
            src_ref=full.at[plane(side * (CZ - 1))], dst_ref=near_rx.at[s, 1 - side],
            send_sem=near_ssem.at[side], recv_sem=near_rsem.at[s, 1 - side],
            device_id=(dn, up)[side], device_id_type=MESH,
        )

    def half_copy(s, side):
        return pltpu.make_async_remote_copy(
            src_ref=half_send.at[side], dst_ref=half_rx.at[s, 1 - side],
            send_sem=half_ssem.at[side], recv_sem=half_rsem.at[s, 1 - side],
            device_id=(dn, up)[side], device_id_type=MESH,
        )

    def rho_copy(which, side):
        return pltpu.make_async_remote_copy(
            src_ref=rho_send.at[which, side], dst_ref=rho_rx.at[which, 1 - side],
            send_sem=rho_ssem.at[which, side], recv_sem=rho_rsem.at[which, 1 - side],
            device_id=(dn, up)[side], device_id_type=MESH,
        )

    def w_copy(s):
        return pltpu.make_async_remote_copy(
            src_ref=w_send, dst_ref=w_rx.at[s], send_sem=w_ssem, recv_sem=w_rsem.at[s],
            device_id=partner, device_id_type=MESH,
        )

    def far_copy(s):
        return pltpu.make_async_remote_copy(
            src_ref=full.at[pl.ds(p * ((CZ - 1) * FULL), N)], dst_ref=far_rx.at[s],
            send_sem=far_ssem, recv_sem=far_rsem.at[s],
            device_id=far_to, device_id_type=MESH,
        )

    plane_parity = (iota((N, N), 0) + iota((N, N), 1)) % 2
    half_parity = (iota((FINE, N), 0) + iota((FINE, N), 1)) % 2
    lane_c = iota((N, N), 1)
    lane_p = iota((HALF, N), 1)
    fine_parity = (lane_p // FINE + lane_p) % 2
    x_first = lane_p % FINE == 0
    x_last = lane_p % FINE == FINE - 1
    y_first = lane_p < FINE

    def folded(cells, parity):
        return jnp.where(half_parity == parity, cells[:FINE], pltpu.roll(cells[FINE:], 1, 1))

    def unfolded(cells):
        return jnp.concatenate([cells, pltpu.roll(cells, N - 1, 1)], axis=0)

    for ref, lead in ((ca, 2), (cb, 2), (halo, 0)):
        for role in range(max(lead, 1)):
            for i in range(PAIRS + 2 if lead else 2):
                where = (role, i) if lead else (i,)
                ref[(*where, slice(0, TOP), slice(None))] = jnp.zeros((TOP, N), jnp.float32)
                ref[(*where, slice(TOP + N, None), slice(None))] = jnp.zeros((TOP, N), jnp.float32)

    def pack_faces():
        lane = iota((CZ, N), 1)
        for whose, dst in ((1 - p, w_send), (p, w_own)):
            packed = jnp.zeros((CZ, N), jnp.float32)
            for k in range(SLOTS):
                ox = anchors[0, whose * SLOTS + k]
                oy = jnp.maximum(anchors[1, whose * SLOTS + k], 1)
                base = k * FINE
                for t in range(WIN):
                    line = full[pl.ds(oy + t, CZ, stride=FULL), :]
                    low = pltpu.roll(line, lax.rem(base + t - (ox - 1) + 2 * N, N), 1)
                    high = pltpu.roll(line, lax.rem(base + WIN + t - (ox + WIN) + 2 * N, N), 1)
                    packed = jnp.where(lane == base + t, low, packed)
                    packed = jnp.where(lane == base + WIN + t, high, packed)
                for kind, row in ((2, oy - 1), (3, oy + WIN)):
                    line = full[pl.ds(row, CZ, stride=FULL), :]
                    line = pltpu.roll(line, lax.rem(base + kind * WIN - ox + 2 * N, N), 1)
                    inside = jnp.logical_and(lane >= base + kind * WIN, lane < base + (kind + 1) * WIN)
                    packed = jnp.where(inside, line, packed)
            dst[...] = packed

    q_start = order[0]
    for z in range(CZ):
        loads[z].wait()
    for i in range(PAIRS):
        even, odd = full[plane(2 * i), :], full[plane(2 * i + 1), :]
        ca[0, i + 1, rows, :] = jnp.where(plane_parity == 0, even, odd)
        ca[1, i + 1, rows, :] = jnp.where(plane_parity == 0, odd, even)
    half_send[0] = folded(full[plane(1), :], q_start)
    half_send[1] = folded(full[plane(CZ - 2), :], 1 - q_start)
    loads[CZ].wait()
    for which in range(2):
        rho_send[which, 0] = folded(raw_rho[0], (q_start + which) % 2)
        rho_send[which, 1] = folded(raw_rho[CZ - 1], (q_start + which + 1) % 2)
    pack_faces()

    pl.semaphore_wait(barrier, sum(ok.astype(jnp.int32) for _, ok in greeted))

    def start_halo(s):
        for make in (near_copy, half_copy):
            for side, ok in sides:
                @pl.when(ok)
                def _(make=make, side=side):
                    make(s, side).start()

    def start_rho(which):
        for side, ok in sides:
            @pl.when(ok)
            def _(side=side):
                rho_copy(which, side).start()

    def start_far(s):
        @pl.when(far_to_ok)
        def _():
            far_copy(s).start()

    start_halo(0)
    start_rho(0)
    start_far(0)
    w_copy(0).start()
    start_rho(1)
    lax.fori_loop(0, HALF, fetch, 0)

    for i in range(PAIRS):
        even, odd = raw_rho[2 * i], raw_rho[2 * i + 1]
        rho_c[0, i] = jnp.where(plane_parity == 0, even, odd)
        rho_c[1, i] = jnp.where(plane_parity == 0, odd, even)

    for slot in range(SLOTS):
        ox = anchors[0, p * SLOTS + slot]
        row, lane = iota((N, N), 0), lane_c
        sx[slot] = (row == ox + (lane % FINE) // 4).astype(jnp.float32).astype(jnp.bfloat16)
        wanted = slot * FINE + jnp.where(lane < FINE, 3 * WIN, 2 * WIN) + (lane % FINE) // 4
        ey[slot] = (row == wanted).astype(jnp.float32).astype(jnp.bfloat16)
    pltpu.make_async_copy(raw_pot, raw_pot, in_sem.at[CZ + 1]).wait()
    pltpu.make_async_copy(raw_src, raw_src, in_sem.at[CZ + 2]).wait()

    def split(j, carry):
        for slot in range(SLOTS):
            for raw, scale, put in ((raw_pot, 4.0, 0), (raw_src, 0.25, 1)):
                even = scale * raw[slot, j, pl.ds(0, HALF, stride=2), :]
                odd = scale * raw[slot, j, pl.ds(1, HALF, stride=2), :]
                zero = jnp.where(fine_parity == 0, even, odd)
                one = jnp.where(fine_parity == 0, odd, even)
                if put == 0:
                    pa[slot, 0, j + 1, pl.ds(TOP, HALF), :] = zero
                    pa[slot, 1, j + 1, pl.ds(TOP, HALF), :] = one
                else:
                    src_c[slot, 0, j] = zero
                    src_c[slot, 1, j] = one
        return carry

    lax.fori_loop(0, HALF, split, 0)

    def coarse_pairs(s, b, first, q, pairs, first_half):
        cur, nxt = bufs[b], bufs[1 - b]
        which = jnp.where(q == q_start, 0, 1)

        def cell(i):
            if i in (0, PAIRS + 1):
                return near_rx[s, i // PAIRS]
            return cur[first if first_half else 1 - first, i, rows, :]

        def other(i, at):
            if not first_half:
                return nxt[0, i, at, :]
            if i in (0, PAIRS + 1):
                return halo[i // PAIRS, at, :]
            return cur[1 - first, i, at, :]

        outs = []
        for i in pairs:
            near = other(i, rows)
            if i == 0:
                second = other(1, rows)
            elif i == PAIRS + 1:
                second = other(PAIRS, rows)
            else:
                second = jnp.where(plane_parity == q, other(i - 1, rows), other(i + 1, rows))
            source = rho_h[which, i // PAIRS] if i in (0, PAIRS + 1) else rho_c[q, i - 1]
            outs.append(
                relaxed(
                    cell(i),
                    (
                        near,
                        second,
                        other(i, pl.ds(TOP - 1, N)),
                        other(i, pl.ds(TOP + 1, N)),
                        jnp.where(lane_c == 0, 0.0, pltpu.roll(near, 1, 1)),
                        jnp.where(lane_c == N - 1, 0.0, pltpu.roll(near, N - 1, 1)),
                    ),
                    source,
                )
            )
        for i, out in zip(pairs, outs):
            nxt[0 if first_half else 1, i, rows, :] = out

    def patch_half(slot, center_ref, role_c, other_ref, role_b, out_ref, role_out, q):
        data = pl.ds(TOP, HALF)

        def step(k, carry):
            j0 = k * JB
            b = [other_ref[slot, role_b, j0 + t, data, :] for t in range(JB + 2)]
            across = [pltpu.roll(jnp.where(y_first, b[t + 1], b[t]), FINE, 1) for t in range(JB + 1)]
            outs = []
            for t in range(JB):
                below = other_ref[slot, role_b, j0 + t + 1, pl.ds(TOP - 1, HALF), :]
                above = other_ref[slot, role_b, j0 + t + 1, pl.ds(TOP + 1, HALF), :]
                face = x_face[k * (JB // 2) + t // 2]
                near = b[t + 1]
                outs.append(
                    relaxed(
                        center_ref[slot, role_c, j0 + t + 1, data, :],
                        (
                            near,
                            jnp.where(fine_parity == q, below, above),
                            across[t],
                            across[t + 1],
                            jnp.where(x_first, face, pltpu.roll(near, 1, 1)),
                            jnp.where(x_last, face, pltpu.roll(near, N - 1, 1)),
                        ),
                        src_c[slot, q, j0 + t],
                    )
                )
            for t in range(JB):
                out_ref[slot, role_out, j0 + t + 1, data, :] = outs[t]
            return carry

        lax.fori_loop(0, HALF // JB, step, 0)

    def faces_of(s, slot, prev, nxt):
        data = pl.ds(TOP, HALF)
        w = 4.0 * w_rows[...]
        for t in range(WIN):
            low = jnp.broadcast_to(w[:, slot * FINE + t : slot * FINE + t + 1], (HALF, N))
            high = jnp.broadcast_to(w[:, slot * FINE + WIN + t : slot * FINE + WIN + t + 1], (HALF, N))
            x_face[t] = jnp.where(x_last, high, low)
        y_face = split_dot(w, ey[slot])
        oy = jnp.maximum(anchors[1, p * SLOTS + slot], 1)
        z_rows = jnp.concatenate([zplanes[0, pl.ds(oy, WIN), :], zplanes[1, pl.ds(oy, WIN), :]], axis=0)
        z_face = split_dot(z_rows, sx[slot])
        for ref, role in ((prev, 0), (prev, 1), (nxt, 0)):
            ref[slot, role, 0, data, :] = y_face
            ref[slot, role, HALF + 1, data, :] = y_face
            for j in range(HALF):
                ref[slot, role, j + 1, TOP - 1 : TOP, :] = z_face[j // 2 : j // 2 + 1]
                ref[slot, role, j + 1, TOP + HALF : TOP + HALF + 1, :] = z_face[WIN + j // 2 : WIN + j // 2 + 1]

    patch_bufs = (pa, pb)

    def sweep(s, b, may_end):
        q = order[s]
        before = order[jnp.maximum(s - 1, 0)]
        first = jnp.where(s == 0, q, jnp.where(q == before, 0, 1))
        cur, nxt = bufs[b], bufs[1 - b]

        def unless_last(do):
            if may_end:
                pl.when(s < SWEEPS - 1)(do)
            else:
                do()

        coarse_pairs(s, b, first, q, (2, PAIRS - 1), True)
        for side, ok in sides:
            @pl.when(ok)
            def _(side=side):
                near_copy(s, 1 - side).wait_recv()
                half_copy(s, 1 - side).wait_recv()
                second = unfolded(half_rx[s, side])
                halo[side, rows, :] = jnp.where(
                    plane_parity == (1 - q if side == 0 else q), second, near_rx[s, side]
                )

                @pl.when(s == b)
                def _():
                    rho_copy(b, 1 - side).wait_recv()
                    rho_h[b, side] = unfolded(rho_rx[b, side])

            @pl.when(jnp.logical_not(ok))
            def _(side=side):
                halo[side, rows, :] = jnp.zeros((N, N), jnp.float32)

        coarse_pairs(s, b, first, q, (1, PAIRS), True)
        coarse_pairs(s, b, first, q, (0, PAIRS + 1), True)
        for side, ok in sides:
            @pl.when(jnp.logical_not(ok))
            def _(side=side):
                nxt[0, side * (PAIRS + 1), rows, :] = jnp.zeros((N, N), jnp.float32)
        coarse_pairs(s, b, first, 1 - q, (1, PAIRS), False)

        for side, ok in sides:
            @pl.when(ok)
            def _(side=side):
                near_copy(s, side).wait_send()
                half_copy(s, side).wait_send()

                @pl.when(s == b)
                def _():
                    rho_copy(b, side).wait_send()

        @pl.when(far_to_ok)
        def _():
            far_copy(s).wait_send()

        w_copy(s).wait_send()

        def whole(z):
            role = z % 2
            i = z // 2 + 1
            return jnp.where(plane_parity == q, nxt[role, i, rows, :], nxt[1 - role, i, rows, :])

        def send_outer():
            full[plane(0), :] = whole(0)
            full[plane(CZ - 1), :] = whole(CZ - 1)
            q_next = order[jnp.minimum(s + 1, SWEEPS - 1)]
            read = jnp.where(q_next == q, 1, 0)
            half_send[0] = folded(nxt[read, 1, rows, :], q_next)
            half_send[1] = folded(nxt[read, PAIRS, rows, :], 1 - q_next)
            start_halo(s + 1)
            start_far(s + 1)

        unless_last(send_outer)
        coarse_pairs(s, b, first, 1 - q, (2, PAIRS - 1), False)

        w_copy(s).wait_recv()
        mine, theirs = w_own[...], w_rx[s]
        lower = jnp.where(p == 0, mine, theirs)
        upper = jnp.where(p == 0, theirs, mine)
        for t in range(2):
            w_rows[pl.ds(t, CZ, stride=2), :] = lower
            w_rows[pl.ds(2 * CZ + t, CZ, stride=2), :] = upper

        def send_faces():
            for z in range(1, CZ - 1):
                full[plane(z), :] = whole(z)
            pack_faces()
            w_copy(s + 1).start()

        unless_last(send_faces)
        if may_end:
            @pl.when(s == SWEEPS - 1)
            def _():
                for z in range(CZ):
                    coarse_stage[z] = whole(z)
                pltpu.make_async_copy(coarse_stage, coarse_hbm, out_sem.at[SLOTS]).start()

        @pl.when(far_from_ok)
        def _():
            far_copy(s).wait_recv()

        near_ok = jnp.where(p == 0, has_dn, has_up)
        zplanes[p] = jnp.where(near_ok, 4.0 * near_rx[s, p], 0.0)
        zplanes[1 - p] = jnp.where(far_from_ok, 4.0 * far_rx[s], 0.0)
        for slot in range(SLOTS):
            now, new = patch_bufs[b], patch_bufs[1 - b]
            faces_of(s, slot, now, new)
            patch_half(slot, now, first, now, 1 - first, new, 0, q)
            patch_half(slot, now, 1 - first, new, 0, new, 1, 1 - q)
            if may_end:
                @pl.when(s == SWEEPS - 1)
                def _(slot=slot, new=new):
                    live = slot < owned[p]

                    def join(j, carry):
                        one = 0.25 * new[slot, 0, j + 1, pl.ds(TOP, HALF), :]
                        two = 0.25 * new[slot, 1, j + 1, pl.ds(TOP, HALF), :]
                        for odd in range(2):
                            z = pl.ds(odd, HALF, stride=2)
                            swept = jnp.where(fine_parity == (q + odd) % 2, one, two)
                            out_stage[slot, j, z, :] = jnp.where(live, swept, raw_pot[slot, j, z, :])
                        pltpu.make_async_copy(
                            out_stage.at[slot, j], patch_hbm.at[slot, :, columns(j)], out_sem.at[slot]
                        ).start()
                        return carry

                    lax.fori_loop(0, HALF, join, 0)

    def two_sweeps(t, carry):
        sweep(2 * t, 0, False)
        sweep(2 * t + 1, 1, True)
        return carry

    lax.fori_loop(0, SWEEPS // 2, two_sweeps, 0)
    pltpu.make_async_copy(coarse_stage, coarse_hbm, out_sem.at[SLOTS]).wait()
    for slot in range(SLOTS):
        pltpu.make_async_copy(out_stage.at[slot], out_stage.at[slot], out_sem.at[slot]).wait()


def on_device(groups, phi, rho, pot, src, anchors, owned, order):
    f32, bf16 = jnp.float32, jnp.bfloat16
    dma = pltpu.SemaphoreType.DMA
    smem = pl.BlockSpec(memory_space=pltpu.SMEM)
    hbm = pl.BlockSpec(memory_space=pltpu.HBM)
    anywhere = pl.BlockSpec(memory_space=pl.ANY)
    return pl.pallas_call(
        functools.partial(kernel, groups),
        out_shape=(pltpu.VMEM(phi.shape, f32), pltpu.VMEM(pot.shape, f32)),
        in_specs=[smem] * 3 + [hbm] * 4,
        out_specs=(anywhere, anywhere),
        scratch_shapes=[
            pltpu.VMEM((CZ * FULL, N), f32),
            pltpu.VMEM((CZ, N, N), f32),
            pltpu.VMEM((SLOTS, HALF, FINE, N), f32),
            pltpu.VMEM((SLOTS, HALF, FINE, N), f32),
            pltpu.VMEM((2, PAIRS + 2, N + 2 * TOP, N), f32),
            pltpu.VMEM((2, PAIRS + 2, N + 2 * TOP, N), f32),
            pltpu.VMEM((2, N + 2 * TOP, N), f32),
            pltpu.VMEM((2, PAIRS, N, N), f32),
            pltpu.VMEM((2, 2, N, N), f32),
            pltpu.VMEM((SWEEPS, 2, N, N), f32),
            pltpu.VMEM((2, FINE, N), f32),
            pltpu.VMEM((SWEEPS, 2, FINE, N), f32),
            pltpu.VMEM((2, 2, FINE, N), f32),
            pltpu.VMEM((2, 2, FINE, N), f32),
            pltpu.VMEM((CZ, N), f32),
            pltpu.VMEM((CZ, N), f32),
            pltpu.VMEM((SWEEPS, CZ, N), f32),
            pltpu.VMEM((SWEEPS, N, N), f32),
            pltpu.VMEM((2, N, N), f32),
            pltpu.VMEM((HALF, N), f32),
            pltpu.VMEM((SLOTS, 2, HALF + 2, HALF + 2 * TOP, N), f32),
            pltpu.VMEM((SLOTS, 2, HALF + 2, HALF + 2 * TOP, N), f32),
            pltpu.VMEM((SLOTS, 2, HALF, HALF, N), f32),
            pltpu.VMEM((WIN, HALF, N), f32),
            pltpu.VMEM((SLOTS, N, N), bf16),
            pltpu.VMEM((SLOTS, N, N), bf16),
            pltpu.VMEM((CZ, N, N), f32),
            pltpu.VMEM((SLOTS, HALF, FINE, N), f32),
            dma((CZ + 3,)),
            dma((SLOTS + 1,)),
            dma((2,)),
            dma((SWEEPS, 2)),
            dma((2,)),
            dma((SWEEPS, 2)),
            dma((2, 2)),
            dma((2, 2)),
            dma,
            dma((SWEEPS,)),
            dma,
            dma((SWEEPS,)),
        ],
        compiler_params=pltpu.CompilerParams(
            collective_id=0, has_side_effects=True, vmem_limit_bytes=54000000
        ),
        name="smooth",
    )(anchors.T, owned, order, phi, rho, pot, src)


def solution(mesh):
    in_specs = (
        P(("slab", "patch"), None, None),
        P(("slab", "patch"), None, None),
        P(("slab", "patch"), None, None),
        P(("slab", "patch"), None, None),
        P("slab", None),
        P("slab"),
        P(),
    )
    out_specs = (P(("slab", "patch"), None, None), P(("slab", "patch"), None, None))
    return jax.shard_map(
        functools.partial(on_device, mesh.shape["slab"]),
        mesh=mesh, in_specs=in_specs, out_specs=out_specs, check_vma=False,
    )
```

```python
import functools

import jax
import jax.numpy as jnp
from jax import lax
from jax.experimental import pallas as pl
from jax.experimental.pallas import tpu as pltpu
from jax.sharding import PartitionSpec as P

MESH = pl.DeviceIdType.MESH
SWEEPS = 4
N = 128
CZ = 8
PAIRS = CZ // 2
SLOTS = 2
FINE = 64
HALF = FINE // 2
WIN = 16
TOP = 8
FULL = N + 8
JOIN = 4
JB = 8


def relaxed(center, neighbours, source):
    r_sum = rv_sum = v_sum = None
    for value in neighbours:
        r = pl.reciprocal(1.0 + jnp.abs(value - center), approx=True)
        rv = r * value
        r_sum = r if r_sum is None else r_sum + r
        rv_sum = rv if rv_sum is None else rv_sum + rv
        v_sum = value if v_sum is None else v_sum + value
    return (rv_sum + (v_sum - source)) * pl.reciprocal(6.0 + r_sum, approx=True)


def iota(shape, dim):
    return lax.broadcasted_iota(jnp.int32, shape, dim)


def split_dot(rows, onehot):
    high = rows.astype(jnp.bfloat16)
    low = (rows - high.astype(jnp.float32)).astype(jnp.bfloat16)
    return jnp.dot(high, onehot, preferred_element_type=jnp.float32) + jnp.dot(
        low, onehot, preferred_element_type=jnp.float32
    )


def kernel(
    groups,
    anchors, owned, order, phi_hbm, rho_hbm, pot_hbm, src_hbm,
    coarse_hbm, patch_hbm,
    full, raw_rho, raw_pot, raw_src,
    ca, cb, halo, rho_c, rho_h, near_rx, near, pair_send, pair_rx, rho_send, rho_rx,
    w_own, w_send, w_rx, far_rx, zplanes, w_rows, pa, pb, src_c, x_face, sx, ey, coarse_stage, out_stage,
    in_sem, out_sem, near_ssem, near_rsem, pair_ssem, pair_rsem, rho_ssem, rho_rsem,
    w_ssem, w_rsem, far_ssem, far_rsem,
):
    g = lax.axis_index("slab")
    p = lax.axis_index("patch")
    has_up = jnp.logical_or(g < groups - 1, p == 0)
    has_dn = jnp.logical_or(g > 0, p == 1)
    far_to_ok = jnp.where(p == 0, g > 0, g < groups - 1)
    far_from_ok = jnp.where(p == 0, g < groups - 1, g > 0)
    wrap = lambda v: lax.rem(v + groups, groups)
    up = (wrap(g + p), 1 - p)
    dn = (wrap(g - 1 + p), 1 - p)
    partner = (g, 1 - p)
    far_to = (wrap(g + 2 * p - 1), p)
    far_from = (wrap(g + 1 - 2 * p), p)
    sides = ((0, has_dn), (1, has_up))

    barrier = pltpu.get_barrier_semaphore()
    greeted = ((up, has_up), (dn, has_dn), (far_to, far_to_ok), (far_from, far_from_ok))
    for device, ok in greeted:
        @pl.when(ok)
        def _(device=device):
            pl.semaphore_signal(barrier, inc=1, device_id=device, device_id_type=MESH)

    def plane(z):
        return pl.ds(z * FULL, N)

    loads = [pltpu.make_async_copy(phi_hbm.at[z], full.at[plane(z)], in_sem.at[z]) for z in range(CZ)]
    loads.append(pltpu.make_async_copy(rho_hbm, raw_rho, in_sem.at[CZ]))
    for load in loads:
        load.start()

    def columns(j):
        return pl.ds(pl.multiple_of(j * N, N), N)

    def fetch(j, carry):
        for slot in range(SLOTS):
            pltpu.make_async_copy(
                pot_hbm.at[slot, :, columns(j)], raw_pot.at[slot, j], in_sem.at[CZ + 1]
            ).start()
            pltpu.make_async_copy(
                src_hbm.at[slot, :, columns(j)], raw_src.at[slot, j], in_sem.at[CZ + 2]
            ).start()
        return carry

    rows = pl.ds(TOP, N)
    bufs = (ca, cb)

    def near_copy(side):
        return pltpu.make_async_remote_copy(
            src_ref=full.at[plane(side * (CZ - 1))], dst_ref=near_rx.at[1 - side],
            send_sem=near_ssem.at[side], recv_sem=near_rsem.at[1 - side],
            device_id=(dn, up)[side], device_id_type=MESH,
        )

    def pair_copy(s, side, at):
        return pltpu.make_async_remote_copy(
            src_ref=pair_send.at[side, at], dst_ref=pair_rx.at[s, 1 - side, at],
            send_sem=pair_ssem.at[side], recv_sem=pair_rsem.at[s, 1 - side],
            device_id=(dn, up)[side], device_id_type=MESH,
        )

    def rho_copy(which, side):
        return pltpu.make_async_remote_copy(
            src_ref=rho_send.at[which, side], dst_ref=rho_rx.at[which, 1 - side],
            send_sem=rho_ssem.at[which, side], recv_sem=rho_rsem.at[which, 1 - side],
            device_id=(dn, up)[side], device_id_type=MESH,
        )

    def w_copy(s):
        return pltpu.make_async_remote_copy(
            src_ref=w_send, dst_ref=w_rx.at[s], send_sem=w_ssem, recv_sem=w_rsem.at[s],
            device_id=partner, device_id_type=MESH,
        )

    def far_copy(s):
        return pltpu.make_async_remote_copy(
            src_ref=full.at[pl.ds(p * ((CZ - 1) * FULL), N)], dst_ref=far_rx.at[s],
            send_sem=far_ssem, recv_sem=far_rsem.at[s],
            device_id=far_to, device_id_type=MESH,
        )

    plane_parity = (iota((N, N), 0) + iota((N, N), 1)) % 2
    half_parity = (iota((FINE, N), 0) + iota((FINE, N), 1)) % 2
    lane_c = iota((N, N), 1)
    lane_p = iota((HALF, N), 1)
    fine_parity = (lane_p // FINE + lane_p) % 2
    x_first = lane_p % FINE == 0
    x_last = lane_p % FINE == FINE - 1
    y_first = lane_p < FINE

    def folded(cells, parity):
        return jnp.where(half_parity == parity, cells[:FINE], pltpu.roll(cells[FINE:], 1, 1))

    def unfolded(cells):
        return jnp.concatenate([cells, pltpu.roll(cells, N - 1, 1)], axis=0)

    for ref, lead in ((ca, 2), (cb, 2), (halo, 0)):
        for role in range(max(lead, 1)):
            for i in range(PAIRS + 2 if lead else 2):
                where = (role, i) if lead else (i,)
                ref[(*where, slice(0, TOP), slice(None))] = jnp.zeros((TOP, N), jnp.float32)
                ref[(*where, slice(TOP + N, None), slice(None))] = jnp.zeros((TOP, N), jnp.float32)

    def pack_faces():
        lane = iota((CZ, N), 1)
        for whose, dst in ((1 - p, w_send), (p, w_own)):
            packed = jnp.zeros((CZ, N), jnp.float32)
            for k in range(SLOTS):
                ox = anchors[0, whose * SLOTS + k]
                oy = jnp.maximum(anchors[1, whose * SLOTS + k], 1)
                base = k * FINE
                for t in range(WIN):
                    line = full[pl.ds(oy + t, CZ, stride=FULL), :]
                    low = pltpu.roll(line, lax.rem(base + t - (ox - 1) + 2 * N, N), 1)
                    high = pltpu.roll(line, lax.rem(base + WIN + t - (ox + WIN) + 2 * N, N), 1)
                    packed = jnp.where(lane == base + t, low, packed)
                    packed = jnp.where(lane == base + WIN + t, high, packed)
                for kind, row in ((2, oy - 1), (3, oy + WIN)):
                    line = full[pl.ds(row, CZ, stride=FULL), :]
                    line = pltpu.roll(line, lax.rem(base + kind * WIN - ox + 2 * N, N), 1)
                    inside = jnp.logical_and(lane >= base + kind * WIN, lane < base + (kind + 1) * WIN)
                    packed = jnp.where(inside, line, packed)
            dst[...] = packed

    q_start = order[0]
    for z in range(CZ):
        loads[z].wait()
    for i in range(PAIRS):
        even, odd = full[plane(2 * i), :], full[plane(2 * i + 1), :]
        ca[0, i + 1, rows, :] = jnp.where(plane_parity == 0, even, odd)
        ca[1, i + 1, rows, :] = jnp.where(plane_parity == 0, odd, even)
    pair_send[0, FINE:, :] = folded(full[plane(1), :], q_start)
    pair_send[1, FINE:, :] = folded(full[plane(CZ - 2), :], 1 - q_start)
    loads[CZ].wait()
    for which in range(2):
        rho_send[which, 0] = folded(raw_rho[0], (q_start + which) % 2)
        rho_send[which, 1] = folded(raw_rho[CZ - 1], (q_start + which + 1) % 2)
    pack_faces()

    pl.semaphore_wait(barrier, sum(ok.astype(jnp.int32) for _, ok in greeted))

    def start_rho(which):
        for side, ok in sides:
            @pl.when(ok)
            def _(side=side):
                rho_copy(which, side).start()

    def start_far(s):
        @pl.when(far_to_ok)
        def _():
            far_copy(s).start()

    both, second_only = pl.ds(0, N), pl.ds(FINE, FINE)
    for side, ok in sides:
        @pl.when(ok)
        def _(side=side):
            near_copy(side).start()
    for side, ok in sides:
        @pl.when(ok)
        def _(side=side):
            pair_copy(0, side, second_only).start()
    start_rho(0)
    start_far(0)
    w_copy(0).start()
    start_rho(1)
    lax.fori_loop(0, HALF, fetch, 0)

    for i in range(PAIRS):
        even, odd = raw_rho[2 * i], raw_rho[2 * i + 1]
        rho_c[0, i] = jnp.where(plane_parity == 0, even, odd)
        rho_c[1, i] = jnp.where(plane_parity == 0, odd, even)

    for slot in range(SLOTS):
        ox = anchors[0, p * SLOTS + slot]
        row, lane = iota((N, N), 0), lane_c
        sx[slot] = (row == ox + (lane % FINE) // 4).astype(jnp.float32).astype(jnp.bfloat16)
        wanted = slot * FINE + jnp.where(lane < FINE, 3 * WIN, 2 * WIN) + (lane % FINE) // 4
        ey[slot] = (row == wanted).astype(jnp.float32).astype(jnp.bfloat16)
    pltpu.make_async_copy(raw_pot, raw_pot, in_sem.at[CZ + 1]).wait()
    pltpu.make_async_copy(raw_src, raw_src, in_sem.at[CZ + 2]).wait()

    def split(j, carry):
        for slot in range(SLOTS):
            for raw, scale, put in ((raw_pot, 4.0, 0), (raw_src, 0.25, 1)):
                even = scale * raw[slot, j, pl.ds(0, HALF, stride=2), :]
                odd = scale * raw[slot, j, pl.ds(1, HALF, stride=2), :]
                zero = jnp.where(fine_parity == 0, even, odd)
                one = jnp.where(fine_parity == 0, odd, even)
                if put == 0:
                    pa[slot, 0, j + 1, pl.ds(TOP, HALF), :] = zero
                    pa[slot, 1, j + 1, pl.ds(TOP, HALF), :] = one
                else:
                    src_c[slot, 0, j] = zero
                    src_c[slot, 1, j] = one
        return carry

    lax.fori_loop(0, HALF, split, 0)

    def coarse_pairs(s, b, first, q, pairs, first_half):
        cur, nxt = bufs[b], bufs[1 - b]
        which = jnp.where(q == q_start, 0, 1)

        def cell(i):
            if i in (0, PAIRS + 1):
                return near[i // PAIRS]
            return cur[first if first_half else 1 - first, i, rows, :]

        def other(i, at):
            if not first_half:
                return nxt[0, i, at, :]
            if i in (0, PAIRS + 1):
                return halo[i // PAIRS, at, :]
            return cur[1 - first, i, at, :]

        outs = []
        for i in pairs:
            here = other(i, rows)
            if i == 0:
                second = other(1, rows)
            elif i == PAIRS + 1:
                second = other(PAIRS, rows)
            else:
                second = jnp.where(plane_parity == q, other(i - 1, rows), other(i + 1, rows))
            source = rho_h[which, i // PAIRS] if i in (0, PAIRS + 1) else rho_c[q, i - 1]
            outs.append(
                relaxed(
                    cell(i),
                    (
                        here,
                        second,
                        other(i, pl.ds(TOP - 1, N)),
                        other(i, pl.ds(TOP + 1, N)),
                        jnp.where(lane_c == 0, 0.0, pltpu.roll(here, 1, 1)),
                        jnp.where(lane_c == N - 1, 0.0, pltpu.roll(here, N - 1, 1)),
                    ),
                    source,
                )
            )
        for i, out in zip(pairs, outs):
            nxt[0 if first_half else 1, i, rows, :] = out

    def patch_half(slot, center_ref, role_c, other_ref, role_b, out_ref, role_out, q):
        data = pl.ds(TOP, HALF)

        def step(k, carry):
            j0 = k * JB
            b = [other_ref[slot, role_b, j0 + t, data, :] for t in range(JB + 2)]
            across = [pltpu.roll(jnp.where(y_first, b[t + 1], b[t]), FINE, 1) for t in range(JB + 1)]
            outs = []
            for t in range(JB):
                below = other_ref[slot, role_b, j0 + t + 1, pl.ds(TOP - 1, HALF), :]
                above = other_ref[slot, role_b, j0 + t + 1, pl.ds(TOP + 1, HALF), :]
                face = x_face[k * (JB // 2) + t // 2]
                near = b[t + 1]
                outs.append(
                    relaxed(
                        center_ref[slot, role_c, j0 + t + 1, data, :],
                        (
                            near,
                            jnp.where(fine_parity == q, below, above),
                            across[t],
                            across[t + 1],
                            jnp.where(x_first, face, pltpu.roll(near, 1, 1)),
                            jnp.where(x_last, face, pltpu.roll(near, N - 1, 1)),
                        ),
                        src_c[slot, q, j0 + t],
                    )
                )
            for t in range(JB):
                out_ref[slot, role_out, j0 + t + 1, data, :] = outs[t]
            return carry

        lax.fori_loop(0, HALF // JB, step, 0)

    def faces_of(s, slot, prev, nxt):
        data = pl.ds(TOP, HALF)
        w = 4.0 * w_rows[...]
        for t in range(WIN):
            low = jnp.broadcast_to(w[:, slot * FINE + t : slot * FINE + t + 1], (HALF, N))
            high = jnp.broadcast_to(w[:, slot * FINE + WIN + t : slot * FINE + WIN + t + 1], (HALF, N))
            x_face[t] = jnp.where(x_last, high, low)
        y_face = split_dot(w, ey[slot])
        oy = jnp.maximum(anchors[1, p * SLOTS + slot], 1)
        z_rows = jnp.concatenate([zplanes[0, pl.ds(oy, WIN), :], zplanes[1, pl.ds(oy, WIN), :]], axis=0)
        z_face = split_dot(z_rows, sx[slot])
        for ref, role in ((prev, 0), (prev, 1), (nxt, 0)):
            ref[slot, role, 0, data, :] = y_face
            ref[slot, role, HALF + 1, data, :] = y_face
            for j in range(HALF):
                ref[slot, role, j + 1, TOP - 1 : TOP, :] = z_face[j // 2 : j // 2 + 1]
                ref[slot, role, j + 1, TOP + HALF : TOP + HALF + 1, :] = z_face[WIN + j // 2 : WIN + j // 2 + 1]

    patch_bufs = (pa, pb)

    def sweep(s, b, may_end):
        q = order[s]
        before = order[jnp.maximum(s - 1, 0)]
        first = jnp.where(s == 0, q, jnp.where(q == before, 0, 1))
        cur, nxt = bufs[b], bufs[1 - b]

        def unless_last(do):
            if may_end:
                pl.when(s < SWEEPS - 1)(do)
            else:
                do()

        coarse_pairs(s, b, first, q, (2, PAIRS - 1), True)
        for side, ok in sides:
            @pl.when(ok)
            def _(side=side):
                def start_of_all():
                    near_copy(1 - side).wait_recv()
                    pair_copy(s, 1 - side, second_only).wait_recv()
                    near[side] = near_rx[side]

                def later():
                    pair_copy(s, 1 - side, both).wait_recv()
                    mine = plane_parity == (1 - before if side == 0 else before)
                    near[side] = jnp.where(
                        mine, cur[0, side * (PAIRS + 1), rows, :], unfolded(pair_rx[s, side, :FINE, :])
                    )

                if b == 0:
                    pl.when(s == 0)(start_of_all)
                    pl.when(s > 0)(later)
                else:
                    later()
                second = unfolded(pair_rx[s, side, FINE:, :])
                halo[side, rows, :] = jnp.where(
                    plane_parity == (1 - q if side == 0 else q), second, near[side]
                )

                @pl.when(s == b)
                def _():
                    rho_copy(b, 1 - side).wait_recv()
                    rho_h[b, side] = unfolded(rho_rx[b, side])

            @pl.when(jnp.logical_not(ok))
            def _(side=side):
                halo[side, rows, :] = jnp.zeros((N, N), jnp.float32)

        coarse_pairs(s, b, first, q, (1, PAIRS), True)
        coarse_pairs(s, b, first, q, (0, PAIRS + 1), True)
        for side, ok in sides:
            @pl.when(jnp.logical_not(ok))
            def _(side=side):
                nxt[0, side * (PAIRS + 1), rows, :] = jnp.zeros((N, N), jnp.float32)
        coarse_pairs(s, b, first, 1 - q, (1, PAIRS), False)

        for side, ok in sides:
            @pl.when(ok)
            def _(side=side):
                if b == 0:
                    @pl.when(s == 0)
                    def _():
                        near_copy(side).wait_send()
                        pair_copy(s, side, second_only).wait_send()

                    @pl.when(s > 0)
                    def _():
                        pair_copy(s, side, both).wait_send()
                else:
                    pair_copy(s, side, both).wait_send()

                @pl.when(s == b)
                def _():
                    rho_copy(b, side).wait_send()

        @pl.when(far_to_ok)
        def _():
            far_copy(s).wait_send()

        w_copy(s).wait_send()

        def whole(z):
            role = z % 2
            i = z // 2 + 1
            return jnp.where(plane_parity == q, nxt[role, i, rows, :], nxt[1 - role, i, rows, :])

        def send_outer():
            q_next = order[jnp.minimum(s + 1, SWEEPS - 1)]
            read = jnp.where(q_next == q, 1, 0)
            for side, ok in sides:
                i = PAIRS if side else 1
                last, ahead = (q, 1 - q_next) if side else (1 - q, q_next)
                pair_send[side, :FINE, :] = folded(nxt[1, i, rows, :], last)
                pair_send[side, FINE:, :] = folded(nxt[read, i, rows, :], ahead)

                @pl.when(ok)
                def _(side=side):
                    pair_copy(s + 1, side, both).start()

            full[plane(0), :] = whole(0)
            full[plane(CZ - 1), :] = whole(CZ - 1)
            start_far(s + 1)

        unless_last(send_outer)
        coarse_pairs(s, b, first, 1 - q, (2, PAIRS - 1), False)

        w_copy(s).wait_recv()
        mine, theirs = w_own[...], w_rx[s]
        lower = jnp.where(p == 0, mine, theirs)
        upper = jnp.where(p == 0, theirs, mine)
        for t in range(2):
            w_rows[pl.ds(t, CZ, stride=2), :] = lower
            w_rows[pl.ds(2 * CZ + t, CZ, stride=2), :] = upper

        def send_faces():
            for z in range(1, CZ - 1):
                full[plane(z), :] = whole(z)
            pack_faces()
            w_copy(s + 1).start()

        unless_last(send_faces)
        if may_end:
            @pl.when(s == SWEEPS - 1)
            def _():
                for z in range(CZ):
                    coarse_stage[z] = whole(z)
                pltpu.make_async_copy(coarse_stage, coarse_hbm, out_sem.at[SLOTS]).start()

        @pl.when(far_from_ok)
        def _():
            far_copy(s).wait_recv()

        near_ok = jnp.where(p == 0, has_dn, has_up)
        zplanes[p] = jnp.where(near_ok, 4.0 * near[p], 0.0)
        zplanes[1 - p] = jnp.where(far_from_ok, 4.0 * far_rx[s], 0.0)
        for slot in range(SLOTS):
            now, new = patch_bufs[b], patch_bufs[1 - b]
            faces_of(s, slot, now, new)
            patch_half(slot, now, first, now, 1 - first, new, 0, q)
            patch_half(slot, now, 1 - first, new, 0, new, 1, 1 - q)
            if may_end:
                @pl.when(s == SWEEPS - 1)
                def _(slot=slot, new=new):
                    live = slot < owned[p]

                    def join(k, carry):
                        joined = []
                        for t in range(JOIN):
                            j = k * JOIN + t
                            one = 0.25 * new[slot, 0, j + 1, pl.ds(TOP, HALF), :]
                            two = 0.25 * new[slot, 1, j + 1, pl.ds(TOP, HALF), :]
                            for odd in range(2):
                                old = raw_pot[slot, j, pl.ds(odd, HALF, stride=2), :]
                                swept = jnp.where(fine_parity == (q + odd) % 2, one, two)
                                joined.append((j, odd, jnp.where(live, swept, old)))
                        for j, odd, cells in joined:
                            out_stage[slot, j, pl.ds(odd, HALF, stride=2), :] = cells
                        for t in range(JOIN):
                            j = k * JOIN + t
                            pltpu.make_async_copy(
                                out_stage.at[slot, j], patch_hbm.at[slot, :, columns(j)], out_sem.at[slot]
                            ).start()
                        return carry

                    lax.fori_loop(0, HALF // JOIN, join, 0)

    def two_sweeps(t, carry):
        sweep(2 * t, 0, False)
        sweep(2 * t + 1, 1, True)
        return carry

    lax.fori_loop(0, SWEEPS // 2, two_sweeps, 0)
    pltpu.make_async_copy(coarse_stage, coarse_hbm, out_sem.at[SLOTS]).wait()
    for slot in range(SLOTS):
        pltpu.make_async_copy(out_stage.at[slot], out_stage.at[slot], out_sem.at[slot]).wait()


def on_device(groups, phi, rho, pot, src, anchors, owned, order):
    f32, bf16 = jnp.float32, jnp.bfloat16
    dma = pltpu.SemaphoreType.DMA
    smem = pl.BlockSpec(memory_space=pltpu.SMEM)
    hbm = pl.BlockSpec(memory_space=pltpu.HBM)
    anywhere = pl.BlockSpec(memory_space=pl.ANY)
    return pl.pallas_call(
        functools.partial(kernel, groups),
        out_shape=(pltpu.VMEM(phi.shape, f32), pltpu.VMEM(pot.shape, f32)),
        in_specs=[smem] * 3 + [hbm] * 4,
        out_specs=(anywhere, anywhere),
        scratch_shapes=[
            pltpu.VMEM((CZ * FULL, N), f32),
            pltpu.VMEM((CZ, N, N), f32),
            pltpu.VMEM((SLOTS, HALF, FINE, N), f32),
            pltpu.VMEM((SLOTS, HALF, FINE, N), f32),
            pltpu.VMEM((2, PAIRS + 2, N + 2 * TOP, N), f32),
            pltpu.VMEM((2, PAIRS + 2, N + 2 * TOP, N), f32),
            pltpu.VMEM((2, N + 2 * TOP, N), f32),
            pltpu.VMEM((2, PAIRS, N, N), f32),
            pltpu.VMEM((2, 2, N, N), f32),
            pltpu.VMEM((2, N, N), f32),
            pltpu.VMEM((2, N, N), f32),
            pltpu.VMEM((2, N, N), f32),
            pltpu.VMEM((SWEEPS, 2, N, N), f32),
            pltpu.VMEM((2, 2, FINE, N), f32),
            pltpu.VMEM((2, 2, FINE, N), f32),
            pltpu.VMEM((CZ, N), f32),
            pltpu.VMEM((CZ, N), f32),
            pltpu.VMEM((SWEEPS, CZ, N), f32),
            pltpu.VMEM((SWEEPS, N, N), f32),
            pltpu.VMEM((2, N, N), f32),
            pltpu.VMEM((HALF, N), f32),
            pltpu.VMEM((SLOTS, 2, HALF + 2, HALF + 2 * TOP, N), f32),
            pltpu.VMEM((SLOTS, 2, HALF + 2, HALF + 2 * TOP, N), f32),
            pltpu.VMEM((SLOTS, 2, HALF, HALF, N), f32),
            pltpu.VMEM((WIN, HALF, N), f32),
            pltpu.VMEM((SLOTS, N, N), bf16),
            pltpu.VMEM((SLOTS, N, N), bf16),
            pltpu.VMEM((CZ, N, N), f32),
            pltpu.VMEM((SLOTS, HALF, FINE, N), f32),
            dma((CZ + 3,)),
            dma((SLOTS + 1,)),
            dma((2,)),
            dma((2,)),
            dma((2,)),
            dma((SWEEPS, 2)),
            dma((2, 2)),
            dma((2, 2)),
            dma,
            dma((SWEEPS,)),
            dma,
            dma((SWEEPS,)),
        ],
        compiler_params=pltpu.CompilerParams(
            collective_id=0, has_side_effects=True, vmem_limit_bytes=54000000
        ),
        name="smooth",
    )(anchors.T, owned, order, phi, rho, pot, src)


def solution(mesh):
    in_specs = (
        P(("slab", "patch"), None, None),
        P(("slab", "patch"), None, None),
        P(("slab", "patch"), None, None),
        P(("slab", "patch"), None, None),
        P("slab", None),
        P("slab"),
        P(),
    )
    out_specs = (P(("slab", "patch"), None, None), P(("slab", "patch"), None, None))
    return jax.shard_map(
        functools.partial(on_device, mesh.shape["slab"]),
        mesh=mesh, in_specs=in_specs, out_specs=out_specs, check_vma=False,
    )
```

```python
import functools

import jax
import jax.numpy as jnp
from jax import lax
from jax.experimental import pallas as pl
from jax.experimental.pallas import tpu as pltpu
from jax.sharding import PartitionSpec as P

MESH = pl.DeviceIdType.MESH
SWEEPS = 4
N = 128
CZ = 8
PAIRS = CZ // 2
SLOTS = 2
FINE = 64
HALF = FINE // 2
WIN = 16
TOP = 8
FULL = N + 8
JOIN = 4
JB = 16


def relaxed(center, neighbours, source):
    r_sum = rv_sum = v_sum = None
    for value in neighbours:
        r = pl.reciprocal(1.0 + jnp.abs(value - center), approx=True)
        rv = r * value
        r_sum = r if r_sum is None else r_sum + r
        rv_sum = rv if rv_sum is None else rv_sum + rv
        v_sum = value if v_sum is None else v_sum + value
    return (rv_sum + (v_sum - source)) * pl.reciprocal(6.0 + r_sum, approx=True)


def iota(shape, dim):
    return lax.broadcasted_iota(jnp.int32, shape, dim)


def split_dot(rows, onehot):
    high = rows.astype(jnp.bfloat16)
    low = (rows - high.astype(jnp.float32)).astype(jnp.bfloat16)
    return jnp.dot(high, onehot, preferred_element_type=jnp.float32) + jnp.dot(
        low, onehot, preferred_element_type=jnp.float32
    )


def kernel(
    groups,
    anchors, owned, order, phi_hbm, rho_hbm, pot_hbm, src_hbm,
    coarse_hbm, patch_hbm,
    full, raw_rho, raw_pot, raw_src,
    ca, cb, halo, rho_c, rho_h, near_rx, near, pair_send, pair_rx, rho_send, rho_rx,
    w_own, w_send, w_rx, far_rx, zplanes, w_rows, pa, pb, src_c, x_face, sx, ey, coarse_stage, out_stage,
    in_sem, out_sem, near_ssem, near_rsem, pair_ssem, pair_rsem, rho_ssem, rho_rsem,
    w_ssem, w_rsem, far_ssem, far_rsem,
):
    g = lax.axis_index("slab")
    p = lax.axis_index("patch")
    has_up = jnp.logical_or(g < groups - 1, p == 0)
    has_dn = jnp.logical_or(g > 0, p == 1)
    far_to_ok = jnp.where(p == 0, g > 0, g < groups - 1)
    far_from_ok = jnp.where(p == 0, g < groups - 1, g > 0)
    wrap = lambda v: lax.rem(v + groups, groups)
    up = (wrap(g + p), 1 - p)
    dn = (wrap(g - 1 + p), 1 - p)
    partner = (g, 1 - p)
    far_to = (wrap(g + 2 * p - 1), p)
    far_from = (wrap(g + 1 - 2 * p), p)
    sides = ((0, has_dn), (1, has_up))

    barrier = pltpu.get_barrier_semaphore()
    greeted = ((up, has_up), (dn, has_dn), (far_to, far_to_ok), (far_from, far_from_ok))
    for device, ok in greeted:
        @pl.when(ok)
        def _(device=device):
            pl.semaphore_signal(barrier, inc=1, device_id=device, device_id_type=MESH)

    def plane(z):
        return pl.ds(z * FULL, N)

    loads = [pltpu.make_async_copy(phi_hbm.at[z], full.at[plane(z)], in_sem.at[z]) for z in range(CZ)]
    loads.append(pltpu.make_async_copy(rho_hbm, raw_rho, in_sem.at[CZ]))
    for load in loads:
        load.start()

    def columns(j):
        return pl.ds(pl.multiple_of(j * N, N), N)

    def fetch(j, carry):
        for slot in range(SLOTS):
            pltpu.make_async_copy(
                pot_hbm.at[slot, :, columns(j)], raw_pot.at[slot, j], in_sem.at[CZ + 1]
            ).start()
            pltpu.make_async_copy(
                src_hbm.at[slot, :, columns(j)], raw_src.at[slot, j], in_sem.at[CZ + 2]
            ).start()
        return carry

    rows = pl.ds(TOP, N)
    bufs = (ca, cb)

    def near_copy(side):
        return pltpu.make_async_remote_copy(
            src_ref=full.at[plane(side * (CZ - 1))], dst_ref=near_rx.at[1 - side],
            send_sem=near_ssem.at[side], recv_sem=near_rsem.at[1 - side],
            device_id=(dn, up)[side], device_id_type=MESH,
        )

    def pair_copy(s, side, at):
        return pltpu.make_async_remote_copy(
            src_ref=pair_send.at[side, at], dst_ref=pair_rx.at[s, 1 - side, at],
            send_sem=pair_ssem.at[side], recv_sem=pair_rsem.at[s, 1 - side],
            device_id=(dn, up)[side], device_id_type=MESH,
        )

    def rho_copy(which, side):
        return pltpu.make_async_remote_copy(
            src_ref=rho_send.at[which, side], dst_ref=rho_rx.at[which, 1 - side],
            send_sem=rho_ssem.at[which, side], recv_sem=rho_rsem.at[which, 1 - side],
            device_id=(dn, up)[side], device_id_type=MESH,
        )

    def w_copy(s):
        return pltpu.make_async_remote_copy(
            src_ref=w_send, dst_ref=w_rx.at[s], send_sem=w_ssem, recv_sem=w_rsem.at[s],
            device_id=partner, device_id_type=MESH,
        )

    def far_copy(s):
        return pltpu.make_async_remote_copy(
            src_ref=full.at[pl.ds(p * ((CZ - 1) * FULL), N)], dst_ref=far_rx.at[s],
            send_sem=far_ssem, recv_sem=far_rsem.at[s],
            device_id=far_to, device_id_type=MESH,
        )

    plane_parity = (iota((N, N), 0) + iota((N, N), 1)) % 2
    half_parity = (iota((FINE, N), 0) + iota((FINE, N), 1)) % 2
    lane_c = iota((N, N), 1)
    lane_p = iota((HALF, N), 1)
    fine_parity = (lane_p // FINE + lane_p) % 2
    x_first = lane_p % FINE == 0
    x_last = lane_p % FINE == FINE - 1
    y_first = lane_p < FINE

    def folded(cells, parity):
        return jnp.where(half_parity == parity, cells[:FINE], pltpu.roll(cells[FINE:], 1, 1))

    def unfolded(cells):
        return jnp.concatenate([cells, pltpu.roll(cells, N - 1, 1)], axis=0)

    for ref, lead in ((ca, 2), (cb, 2), (halo, 0)):
        for role in range(max(lead, 1)):
            for i in range(PAIRS + 2 if lead else 2):
                where = (role, i) if lead else (i,)
                ref[(*where, slice(0, TOP), slice(None))] = jnp.zeros((TOP, N), jnp.float32)
                ref[(*where, slice(TOP + N, None), slice(None))] = jnp.zeros((TOP, N), jnp.float32)

    def pack_faces():
        lane = iota((CZ, N), 1)
        for whose, dst in ((1 - p, w_send), (p, w_own)):
            packed = jnp.zeros((CZ, N), jnp.float32)
            for k in range(SLOTS):
                ox = anchors[0, whose * SLOTS + k]
                oy = jnp.maximum(anchors[1, whose * SLOTS + k], 1)
                base = k * FINE
                for t in range(WIN):
                    line = full[pl.ds(oy + t, CZ, stride=FULL), :]
                    low = pltpu.roll(line, lax.rem(base + t - (ox - 1) + 2 * N, N), 1)
                    high = pltpu.roll(line, lax.rem(base + WIN + t - (ox + WIN) + 2 * N, N), 1)
                    packed = jnp.where(lane == base + t, low, packed)
                    packed = jnp.where(lane == base + WIN + t, high, packed)
                for kind, row in ((2, oy - 1), (3, oy + WIN)):
                    line = full[pl.ds(row, CZ, stride=FULL), :]
                    line = pltpu.roll(line, lax.rem(base + kind * WIN - ox + 2 * N, N), 1)
                    inside = jnp.logical_and(lane >= base + kind * WIN, lane < base + (kind + 1) * WIN)
                    packed = jnp.where(inside, line, packed)
            dst[...] = packed

    q_start = order[0]
    for z in range(CZ):
        loads[z].wait()
    for i in range(PAIRS):
        even, odd = full[plane(2 * i), :], full[plane(2 * i + 1), :]
        ca[0, i + 1, rows, :] = jnp.where(plane_parity == 0, even, odd)
        ca[1, i + 1, rows, :] = jnp.where(plane_parity == 0, odd, even)
    pair_send[0, FINE:, :] = folded(full[plane(1), :], q_start)
    pair_send[1, FINE:, :] = folded(full[plane(CZ - 2), :], 1 - q_start)
    loads[CZ].wait()
    for which in range(2):
        rho_send[which, 0] = folded(raw_rho[0], (q_start + which) % 2)
        rho_send[which, 1] = folded(raw_rho[CZ - 1], (q_start + which + 1) % 2)
    pack_faces()

    pl.semaphore_wait(barrier, sum(ok.astype(jnp.int32) for _, ok in greeted))

    def start_rho(which):
        for side, ok in sides:
            @pl.when(ok)
            def _(side=side):
                rho_copy(which, side).start()

    def start_far(s):
        @pl.when(far_to_ok)
        def _():
            far_copy(s).start()

    both, second_only = pl.ds(0, N), pl.ds(FINE, FINE)
    for side, ok in sides:
        @pl.when(ok)
        def _(side=side):
            near_copy(side).start()
    for side, ok in sides:
        @pl.when(ok)
        def _(side=side):
            pair_copy(0, side, second_only).start()
    start_rho(0)
    start_far(0)
    w_copy(0).start()
    start_rho(1)
    lax.fori_loop(0, HALF, fetch, 0)

    for i in range(PAIRS):
        even, odd = raw_rho[2 * i], raw_rho[2 * i + 1]
        rho_c[0, i] = jnp.where(plane_parity == 0, even, odd)
        rho_c[1, i] = jnp.where(plane_parity == 0, odd, even)

    for slot in range(SLOTS):
        ox = anchors[0, p * SLOTS + slot]
        row, lane = iota((N, N), 0), lane_c
        sx[slot] = (row == ox + (lane % FINE) // 4).astype(jnp.float32).astype(jnp.bfloat16)
        wanted = slot * FINE + jnp.where(lane < FINE, 3 * WIN, 2 * WIN) + (lane % FINE) // 4
        ey[slot] = (row == wanted).astype(jnp.float32).astype(jnp.bfloat16)
    pltpu.make_async_copy(raw_pot, raw_pot, in_sem.at[CZ + 1]).wait()
    pltpu.make_async_copy(raw_src, raw_src, in_sem.at[CZ + 2]).wait()

    def split(j, carry):
        for slot in range(SLOTS):
            for raw, scale, put in ((raw_pot, 4.0, 0), (raw_src, 0.25, 1)):
                even = scale * raw[slot, j, pl.ds(0, HALF, stride=2), :]
                odd = scale * raw[slot, j, pl.ds(1, HALF, stride=2), :]
                zero = jnp.where(fine_parity == 0, even, odd)
                one = jnp.where(fine_parity == 0, odd, even)
                if put == 0:
                    pa[slot, 0, j + 1, pl.ds(TOP, HALF), :] = zero
                    pa[slot, 1, j + 1, pl.ds(TOP, HALF), :] = one
                else:
                    src_c[slot, 0, j] = zero
                    src_c[slot, 1, j] = one
        return carry

    lax.fori_loop(0, HALF, split, 0)

    def coarse_pairs(s, b, first, q, pairs, first_half):
        cur, nxt = bufs[b], bufs[1 - b]
        which = jnp.where(q == q_start, 0, 1)

        def cell(i):
            if i in (0, PAIRS + 1):
                return near[i // PAIRS]
            return cur[first if first_half else 1 - first, i, rows, :]

        def other(i, at):
            if not first_half:
                return nxt[0, i, at, :]
            if i in (0, PAIRS + 1):
                return halo[i // PAIRS, at, :]
            return cur[1 - first, i, at, :]

        outs = []
        for i in pairs:
            here = other(i, rows)
            if i == 0:
                second = other(1, rows)
            elif i == PAIRS + 1:
                second = other(PAIRS, rows)
            else:
                second = jnp.where(plane_parity == q, other(i - 1, rows), other(i + 1, rows))
            source = rho_h[which, i // PAIRS] if i in (0, PAIRS + 1) else rho_c[q, i - 1]
            outs.append(
                relaxed(
                    cell(i),
                    (
                        here,
                        second,
                        other(i, pl.ds(TOP - 1, N)),
                        other(i, pl.ds(TOP + 1, N)),
                        jnp.where(lane_c == 0, 0.0, pltpu.roll(here, 1, 1)),
                        jnp.where(lane_c == N - 1, 0.0, pltpu.roll(here, N - 1, 1)),
                    ),
                    source,
                )
            )
        for i, out in zip(pairs, outs):
            nxt[0 if first_half else 1, i, rows, :] = out

    def patch_half(slot, center_ref, role_c, other_ref, role_b, out_ref, role_out, q):
        data = pl.ds(TOP, HALF)

        def step(k, carry):
            j0 = k * JB
            b = [other_ref[slot, role_b, j0 + t, data, :] for t in range(JB + 2)]
            across = [pltpu.roll(jnp.where(y_first, b[t + 1], b[t]), FINE, 1) for t in range(JB + 1)]
            outs = []
            for t in range(JB):
                below = other_ref[slot, role_b, j0 + t + 1, pl.ds(TOP - 1, HALF), :]
                above = other_ref[slot, role_b, j0 + t + 1, pl.ds(TOP + 1, HALF), :]
                face = x_face[slot, k * (JB // 2) + t // 2]
                near = b[t + 1]
                outs.append(
                    relaxed(
                        center_ref[slot, role_c, j0 + t + 1, data, :],
                        (
                            near,
                            jnp.where(fine_parity == q, below, above),
                            across[t],
                            across[t + 1],
                            jnp.where(x_first, face, pltpu.roll(near, 1, 1)),
                            jnp.where(x_last, face, pltpu.roll(near, N - 1, 1)),
                        ),
                        src_c[slot, q, j0 + t],
                    )
                )
            for t in range(JB):
                out_ref[slot, role_out, j0 + t + 1, data, :] = outs[t]
            return carry

        lax.fori_loop(0, HALF // JB, step, 0)

    def set_faces(prev, nxt):
        data = pl.ds(TOP, HALF)
        pitch = HALF + 2 * TOP
        w = 4.0 * w_rows[...]
        y_faces, z_faces = [], []
        for slot in range(SLOTS):
            y_faces.append(split_dot(w, ey[slot]))
            oy = jnp.maximum(anchors[1, p * SLOTS + slot], 1)
            z_rows = jnp.concatenate([zplanes[0, pl.ds(oy, WIN), :], zplanes[1, pl.ds(oy, WIN), :]], axis=0)
            z_faces.append(split_dot(z_rows, sx[slot]))
        for slot in range(SLOTS):
            for t in range(WIN):
                at = slot * FINE + t
                low = jnp.broadcast_to(w[:, at : at + 1], (HALF, N))
                high = jnp.broadcast_to(w[:, at + WIN : at + WIN + 1], (HALF, N))
                x_face[slot, t] = jnp.where(x_last, high, low)
        for slot in range(SLOTS):
            for ref, role in ((prev, 0), (prev, 1), (nxt, 0)):
                ref[slot, role, 0, data, :] = y_faces[slot]
                ref[slot, role, HALF + 1, data, :] = y_faces[slot]
                lines = ref.reshape(SLOTS * 2 * (HALF + 2) * pitch, N)
                start = (slot * 2 + role) * (HALF + 2) * pitch
                for t in range(2):
                    low = pl.ds(start + (t + 1) * pitch + TOP - 1, WIN, stride=2 * pitch)
                    high = pl.ds(start + (t + 1) * pitch + TOP + HALF, WIN, stride=2 * pitch)
                    lines[low, :] = z_faces[slot][:WIN]
                    lines[high, :] = z_faces[slot][WIN:]

    patch_bufs = (pa, pb)

    def sweep(s, b, may_end):
        q = order[s]
        before = order[jnp.maximum(s - 1, 0)]
        first = jnp.where(s == 0, q, jnp.where(q == before, 0, 1))
        cur, nxt = bufs[b], bufs[1 - b]

        def unless_last(do):
            if may_end:
                pl.when(s < SWEEPS - 1)(do)
            else:
                do()

        coarse_pairs(s, b, first, q, (2, PAIRS - 1), True)
        for side, ok in sides:
            @pl.when(ok)
            def _(side=side):
                def start_of_all():
                    near_copy(1 - side).wait_recv()
                    pair_copy(s, 1 - side, second_only).wait_recv()
                    near[side] = near_rx[side]

                def later():
                    pair_copy(s, 1 - side, both).wait_recv()
                    mine = plane_parity == (1 - before if side == 0 else before)
                    near[side] = jnp.where(
                        mine, cur[0, side * (PAIRS + 1), rows, :], unfolded(pair_rx[s, side, :FINE, :])
                    )

                if b == 0:
                    pl.when(s == 0)(start_of_all)
                    pl.when(s > 0)(later)
                else:
                    later()
                second = unfolded(pair_rx[s, side, FINE:, :])
                halo[side, rows, :] = jnp.where(
                    plane_parity == (1 - q if side == 0 else q), second, near[side]
                )

                @pl.when(s == b)
                def _():
                    rho_copy(b, 1 - side).wait_recv()
                    rho_h[b, side] = unfolded(rho_rx[b, side])

            @pl.when(jnp.logical_not(ok))
            def _(side=side):
                halo[side, rows, :] = jnp.zeros((N, N), jnp.float32)

        coarse_pairs(s, b, first, q, (1, PAIRS), True)
        coarse_pairs(s, b, first, q, (0, PAIRS + 1), True)
        for side, ok in sides:
            @pl.when(jnp.logical_not(ok))
            def _(side=side):
                nxt[0, side * (PAIRS + 1), rows, :] = jnp.zeros((N, N), jnp.float32)
        coarse_pairs(s, b, first, 1 - q, (1, PAIRS), False)

        for side, ok in sides:
            @pl.when(ok)
            def _(side=side):
                if b == 0:
                    @pl.when(s == 0)
                    def _():
                        near_copy(side).wait_send()
                        pair_copy(s, side, second_only).wait_send()

                    @pl.when(s > 0)
                    def _():
                        pair_copy(s, side, both).wait_send()
                else:
                    pair_copy(s, side, both).wait_send()

                @pl.when(s == b)
                def _():
                    rho_copy(b, side).wait_send()

        @pl.when(far_to_ok)
        def _():
            far_copy(s).wait_send()

        w_copy(s).wait_send()

        def whole(z):
            role = z % 2
            i = z // 2 + 1
            return jnp.where(plane_parity == q, nxt[role, i, rows, :], nxt[1 - role, i, rows, :])

        def send_outer():
            q_next = order[jnp.minimum(s + 1, SWEEPS - 1)]
            read = jnp.where(q_next == q, 1, 0)
            for side, ok in sides:
                i = PAIRS if side else 1
                last, ahead = (q, 1 - q_next) if side else (1 - q, q_next)
                pair_send[side, :FINE, :] = folded(nxt[1, i, rows, :], last)
                pair_send[side, FINE:, :] = folded(nxt[read, i, rows, :], ahead)

                @pl.when(ok)
                def _(side=side):
                    pair_copy(s + 1, side, both).start()

            full[plane(0), :] = whole(0)
            full[plane(CZ - 1), :] = whole(CZ - 1)
            start_far(s + 1)

        unless_last(send_outer)
        coarse_pairs(s, b, first, 1 - q, (2, PAIRS - 1), False)

        w_copy(s).wait_recv()
        mine, theirs = w_own[...], w_rx[s]
        lower = jnp.where(p == 0, mine, theirs)
        upper = jnp.where(p == 0, theirs, mine)
        for t in range(2):
            w_rows[pl.ds(t, CZ, stride=2), :] = lower
            w_rows[pl.ds(2 * CZ + t, CZ, stride=2), :] = upper

        def send_faces():
            for z in range(1, CZ - 1):
                full[plane(z), :] = whole(z)
            pack_faces()
            w_copy(s + 1).start()

        unless_last(send_faces)
        if may_end:
            @pl.when(s == SWEEPS - 1)
            def _():
                for z in range(CZ):
                    coarse_stage[z] = whole(z)
                pltpu.make_async_copy(coarse_stage, coarse_hbm, out_sem.at[SLOTS]).start()

        @pl.when(far_from_ok)
        def _():
            far_copy(s).wait_recv()

        near_ok = jnp.where(p == 0, has_dn, has_up)
        zplanes[p] = jnp.where(near_ok, 4.0 * near[p], 0.0)
        zplanes[1 - p] = jnp.where(far_from_ok, 4.0 * far_rx[s], 0.0)
        now, new = patch_bufs[b], patch_bufs[1 - b]
        set_faces(now, new)
        for slot in range(SLOTS):
            patch_half(slot, now, first, now, 1 - first, new, 0, q)
            patch_half(slot, now, 1 - first, new, 0, new, 1, 1 - q)
            if may_end:
                @pl.when(s == SWEEPS - 1)
                def _(slot=slot, new=new):
                    live = slot < owned[p]

                    def join(k, carry):
                        joined = []
                        for t in range(JOIN):
                            j = k * JOIN + t
                            one = 0.25 * new[slot, 0, j + 1, pl.ds(TOP, HALF), :]
                            two = 0.25 * new[slot, 1, j + 1, pl.ds(TOP, HALF), :]
                            for odd in range(2):
                                old = raw_pot[slot, j, pl.ds(odd, HALF, stride=2), :]
                                swept = jnp.where(fine_parity == (q + odd) % 2, one, two)
                                joined.append((j, odd, jnp.where(live, swept, old)))
                        for j, odd, cells in joined:
                            out_stage[slot, j, pl.ds(odd, HALF, stride=2), :] = cells
                        for t in range(JOIN):
                            j = k * JOIN + t
                            pltpu.make_async_copy(
                                out_stage.at[slot, j], patch_hbm.at[slot, :, columns(j)], out_sem.at[slot]
                            ).start()
                        return carry

                    lax.fori_loop(0, HALF // JOIN, join, 0)

    def two_sweeps(t, carry):
        sweep(2 * t, 0, False)
        sweep(2 * t + 1, 1, True)
        return carry

    lax.fori_loop(0, SWEEPS // 2, two_sweeps, 0)
    pltpu.make_async_copy(coarse_stage, coarse_hbm, out_sem.at[SLOTS]).wait()
    for slot in range(SLOTS):
        pltpu.make_async_copy(out_stage.at[slot], out_stage.at[slot], out_sem.at[slot]).wait()


def on_device(groups, phi, rho, pot, src, anchors, owned, order):
    f32, bf16 = jnp.float32, jnp.bfloat16
    dma = pltpu.SemaphoreType.DMA
    smem = pl.BlockSpec(memory_space=pltpu.SMEM)
    hbm = pl.BlockSpec(memory_space=pltpu.HBM)
    anywhere = pl.BlockSpec(memory_space=pl.ANY)
    return pl.pallas_call(
        functools.partial(kernel, groups),
        out_shape=(pltpu.VMEM(phi.shape, f32), pltpu.VMEM(pot.shape, f32)),
        in_specs=[smem] * 3 + [hbm] * 4,
        out_specs=(anywhere, anywhere),
        scratch_shapes=[
            pltpu.VMEM((CZ * FULL, N), f32),
            pltpu.VMEM((CZ, N, N), f32),
            pltpu.VMEM((SLOTS, HALF, FINE, N), f32),
            pltpu.VMEM((SLOTS, HALF, FINE, N), f32),
            pltpu.VMEM((2, PAIRS + 2, N + 2 * TOP, N), f32),
            pltpu.VMEM((2, PAIRS + 2, N + 2 * TOP, N), f32),
            pltpu.VMEM((2, N + 2 * TOP, N), f32),
            pltpu.VMEM((2, PAIRS, N, N), f32),
            pltpu.VMEM((2, 2, N, N), f32),
            pltpu.VMEM((2, N, N), f32),
            pltpu.VMEM((2, N, N), f32),
            pltpu.VMEM((2, N, N), f32),
            pltpu.VMEM((SWEEPS, 2, N, N), f32),
            pltpu.VMEM((2, 2, FINE, N), f32),
            pltpu.VMEM((2, 2, FINE, N), f32),
            pltpu.VMEM((CZ, N), f32),
            pltpu.VMEM((CZ, N), f32),
            pltpu.VMEM((SWEEPS, CZ, N), f32),
            pltpu.VMEM((SWEEPS, N, N), f32),
            pltpu.VMEM((2, N, N), f32),
            pltpu.VMEM((HALF, N), f32),
            pltpu.VMEM((SLOTS, 2, HALF + 2, HALF + 2 * TOP, N), f32),
            pltpu.VMEM((SLOTS, 2, HALF + 2, HALF + 2 * TOP, N), f32),
            pltpu.VMEM((SLOTS, 2, HALF, HALF, N), f32),
            pltpu.VMEM((SLOTS, WIN, HALF, N), f32),
            pltpu.VMEM((SLOTS, N, N), bf16),
            pltpu.VMEM((SLOTS, N, N), bf16),
            pltpu.VMEM((CZ, N, N), f32),
            pltpu.VMEM((SLOTS, HALF, FINE, N), f32),
            dma((CZ + 3,)),
            dma((SLOTS + 1,)),
            dma((2,)),
            dma((2,)),
            dma((2,)),
            dma((SWEEPS, 2)),
            dma((2, 2)),
            dma((2, 2)),
            dma,
            dma((SWEEPS,)),
            dma,
            dma((SWEEPS,)),
        ],
        compiler_params=pltpu.CompilerParams(
            collective_id=0, has_side_effects=True, vmem_limit_bytes=54000000
        ),
        name="smooth",
    )(anchors.T, owned, order, phi, rho, pot, src)


def solution(mesh):
    in_specs = (
        P(("slab", "patch"), None, None),
        P(("slab", "patch"), None, None),
        P(("slab", "patch"), None, None),
        P(("slab", "patch"), None, None),
        P("slab", None),
        P("slab"),
        P(),
    )
    out_specs = (P(("slab", "patch"), None, None), P(("slab", "patch"), None, None))
    return jax.shard_map(
        functools.partial(on_device, mesh.shape["slab"]),
        mesh=mesh, in_specs=in_specs, out_specs=out_specs, check_vma=False,
    )
```

```python
import functools

import jax
import jax.numpy as jnp
from jax import lax
from jax.experimental import pallas as pl
from jax.experimental.pallas import tpu as pltpu
from jax.sharding import PartitionSpec as P

MESH = pl.DeviceIdType.MESH
SWEEPS = 4
N = 128
CZ = 8
PAIRS = CZ // 2
SLOTS = 2
FINE = 64
HALF = FINE // 2
WIN = 16
TOP = 8
FULL = N + 8
JOIN = 4
JB = 32


def relaxed(center, neighbours, source):
    r_sum = rv_sum = v_sum = None
    for value in neighbours:
        r = pl.reciprocal(1.0 + jnp.abs(value - center), approx=True)
        rv = r * value
        r_sum = r if r_sum is None else r_sum + r
        rv_sum = rv if rv_sum is None else rv_sum + rv
        v_sum = value if v_sum is None else v_sum + value
    return (rv_sum + (v_sum - source)) * pl.reciprocal(6.0 + r_sum, approx=True)


def iota(shape, dim):
    return lax.broadcasted_iota(jnp.int32, shape, dim)


def split_dot(rows, onehot):
    high = rows.astype(jnp.bfloat16)
    low = (rows - high.astype(jnp.float32)).astype(jnp.bfloat16)
    return jnp.dot(high, onehot, preferred_element_type=jnp.float32) + jnp.dot(
        low, onehot, preferred_element_type=jnp.float32
    )


def kernel(
    groups,
    anchors, owned, order, phi_hbm, rho_hbm, pot_hbm, src_hbm,
    coarse_hbm, patch_hbm,
    full, raw_rho, raw_pot, raw_src,
    ca, cb, halo, rho_c, rho_h, near_rx, near, pair_send, pair_rx, rho_send, rho_rx,
    w_own, w_send, w_rx, far_rx, zplanes, w_rows, pa, pb, src_c, x_face, sx, ey, coarse_stage, out_stage,
    in_sem, out_sem, near_ssem, near_rsem, pair_ssem, pair_rsem, rho_ssem, rho_rsem,
    w_ssem, w_rsem, far_ssem, far_rsem,
):
    g = lax.axis_index("slab")
    p = lax.axis_index("patch")
    has_up = jnp.logical_or(g < groups - 1, p == 0)
    has_dn = jnp.logical_or(g > 0, p == 1)
    far_to_ok = jnp.where(p == 0, g > 0, g < groups - 1)
    far_from_ok = jnp.where(p == 0, g < groups - 1, g > 0)
    wrap = lambda v: lax.rem(v + groups, groups)
    up = (wrap(g + p), 1 - p)
    dn = (wrap(g - 1 + p), 1 - p)
    partner = (g, 1 - p)
    far_to = (wrap(g + 2 * p - 1), p)
    far_from = (wrap(g + 1 - 2 * p), p)
    sides = ((0, has_dn), (1, has_up))

    barrier = pltpu.get_barrier_semaphore()
    greeted = ((up, has_up), (dn, has_dn), (far_to, far_to_ok), (far_from, far_from_ok))
    for device, ok in greeted:
        @pl.when(ok)
        def _(device=device):
            pl.semaphore_signal(barrier, inc=1, device_id=device, device_id_type=MESH)

    def plane(z):
        return pl.ds(z * FULL, N)

    loads = [pltpu.make_async_copy(phi_hbm.at[z], full.at[plane(z)], in_sem.at[z]) for z in range(CZ)]
    loads.append(pltpu.make_async_copy(rho_hbm, raw_rho, in_sem.at[CZ]))
    for load in loads:
        load.start()

    def columns(j):
        return pl.ds(pl.multiple_of(j * N, N), N)

    def fetch(j, carry):
        for slot in range(SLOTS):
            pltpu.make_async_copy(
                pot_hbm.at[slot, :, columns(j)], raw_pot.at[slot, j], in_sem.at[CZ + 1]
            ).start()
            pltpu.make_async_copy(
                src_hbm.at[slot, :, columns(j)], raw_src.at[slot, j], in_sem.at[CZ + 2]
            ).start()
        return carry

    rows = pl.ds(TOP, N)
    bufs = (ca, cb)

    def near_copy(side):
        return pltpu.make_async_remote_copy(
            src_ref=full.at[plane(side * (CZ - 1))], dst_ref=near_rx.at[1 - side],
            send_sem=near_ssem.at[side], recv_sem=near_rsem.at[1 - side],
            device_id=(dn, up)[side], device_id_type=MESH,
        )

    def pair_copy(s, side, at):
        return pltpu.make_async_remote_copy(
            src_ref=pair_send.at[side, at], dst_ref=pair_rx.at[s, 1 - side, at],
            send_sem=pair_ssem.at[side], recv_sem=pair_rsem.at[s, 1 - side],
            device_id=(dn, up)[side], device_id_type=MESH,
        )

    def rho_copy(which, side):
        return pltpu.make_async_remote_copy(
            src_ref=rho_send.at[which, side], dst_ref=rho_rx.at[which, 1 - side],
            send_sem=rho_ssem.at[which, side], recv_sem=rho_rsem.at[which, 1 - side],
            device_id=(dn, up)[side], device_id_type=MESH,
        )

    def w_copy(s):
        return pltpu.make_async_remote_copy(
            src_ref=w_send, dst_ref=w_rx.at[s], send_sem=w_ssem, recv_sem=w_rsem.at[s],
            device_id=partner, device_id_type=MESH,
        )

    def far_copy(s):
        return pltpu.make_async_remote_copy(
            src_ref=full.at[pl.ds(p * ((CZ - 1) * FULL), N)], dst_ref=far_rx.at[s],
            send_sem=far_ssem, recv_sem=far_rsem.at[s],
            device_id=far_to, device_id_type=MESH,
        )

    plane_parity = (iota((N, N), 0) + iota((N, N), 1)) % 2
    half_parity = (iota((FINE, N), 0) + iota((FINE, N), 1)) % 2
    lane_c = iota((N, N), 1)
    lane_p = iota((HALF, N), 1)
    fine_parity = (lane_p // FINE + lane_p) % 2
    x_first = lane_p % FINE == 0
    x_last = lane_p % FINE == FINE - 1
    y_first = lane_p < FINE

    def folded(cells, parity):
        return jnp.where(half_parity == parity, cells[:FINE], pltpu.roll(cells[FINE:], 1, 1))

    def unfolded(cells):
        return jnp.concatenate([cells, pltpu.roll(cells, N - 1, 1)], axis=0)

    for ref, lead in ((ca, 2), (cb, 2), (halo, 0)):
        for role in range(max(lead, 1)):
            for i in range(PAIRS + 2 if lead else 2):
                where = (role, i) if lead else (i,)
                ref[(*where, slice(0, TOP), slice(None))] = jnp.zeros((TOP, N), jnp.float32)
                ref[(*where, slice(TOP + N, None), slice(None))] = jnp.zeros((TOP, N), jnp.float32)

    def pack_faces():
        lane = iota((CZ, N), 1)
        for whose, dst in ((1 - p, w_send), (p, w_own)):
            packed = jnp.zeros((CZ, N), jnp.float32)
            for k in range(SLOTS):
                ox = anchors[0, whose * SLOTS + k]
                oy = jnp.maximum(anchors[1, whose * SLOTS + k], 1)
                base = k * FINE
                for t in range(WIN):
                    line = full[pl.ds(oy + t, CZ, stride=FULL), :]
                    low = pltpu.roll(line, lax.rem(base + t - (ox - 1) + 2 * N, N), 1)
                    high = pltpu.roll(line, lax.rem(base + WIN + t - (ox + WIN) + 2 * N, N), 1)
                    packed = jnp.where(lane == base + t, low, packed)
                    packed = jnp.where(lane == base + WIN + t, high, packed)
                for kind, row in ((2, oy - 1), (3, oy + WIN)):
                    line = full[pl.ds(row, CZ, stride=FULL), :]
                    line = pltpu.roll(line, lax.rem(base + kind * WIN - ox + 2 * N, N), 1)
                    inside = jnp.logical_and(lane >= base + kind * WIN, lane < base + (kind + 1) * WIN)
                    packed = jnp.where(inside, line, packed)
            dst[...] = packed

    q_start = order[0]
    for z in range(CZ):
        loads[z].wait()
    for i in range(PAIRS):
        even, odd = full[plane(2 * i), :], full[plane(2 * i + 1), :]
        ca[0, i + 1, rows, :] = jnp.where(plane_parity == 0, even, odd)
        ca[1, i + 1, rows, :] = jnp.where(plane_parity == 0, odd, even)
    pair_send[0, FINE:, :] = folded(full[plane(1), :], q_start)
    pair_send[1, FINE:, :] = folded(full[plane(CZ - 2), :], 1 - q_start)
    loads[CZ].wait()
    for which in range(2):
        rho_send[which, 0] = folded(raw_rho[0], (q_start + which) % 2)
        rho_send[which, 1] = folded(raw_rho[CZ - 1], (q_start + which + 1) % 2)

    pl.semaphore_wait(barrier, sum(ok.astype(jnp.int32) for _, ok in greeted))

    def start_rho(which):
        for side, ok in sides:
            @pl.when(ok)
            def _(side=side):
                rho_copy(which, side).start()

    def start_far(s):
        @pl.when(far_to_ok)
        def _():
            far_copy(s).start()

    both, second_only = pl.ds(0, N), pl.ds(FINE, FINE)
    for side, ok in sides:
        @pl.when(ok)
        def _(side=side):
            near_copy(side).start()
    for side, ok in sides:
        @pl.when(ok)
        def _(side=side):
            pair_copy(0, side, second_only).start()
    start_rho(0)
    start_far(0)
    start_rho(1)
    pack_faces()
    w_copy(0).start()
    lax.fori_loop(0, HALF, fetch, 0)

    for i in range(PAIRS):
        even, odd = raw_rho[2 * i], raw_rho[2 * i + 1]
        rho_c[0, i] = jnp.where(plane_parity == 0, even, odd)
        rho_c[1, i] = jnp.where(plane_parity == 0, odd, even)

    for slot in range(SLOTS):
        ox = anchors[0, p * SLOTS + slot]
        row, lane = iota((N, N), 0), lane_c
        sx[slot] = (row == ox + (lane % FINE) // 4).astype(jnp.float32).astype(jnp.bfloat16)
        wanted = slot * FINE + jnp.where(lane < FINE, 3 * WIN, 2 * WIN) + (lane % FINE) // 4
        ey[slot] = (row == wanted).astype(jnp.float32).astype(jnp.bfloat16)
    pltpu.make_async_copy(raw_pot, raw_pot, in_sem.at[CZ + 1]).wait()
    pltpu.make_async_copy(raw_src, raw_src, in_sem.at[CZ + 2]).wait()

    def split(j, carry):
        for slot in range(SLOTS):
            for raw, scale, put in ((raw_pot, 4.0, 0), (raw_src, 0.25, 1)):
                even = scale * raw[slot, j, pl.ds(0, HALF, stride=2), :]
                odd = scale * raw[slot, j, pl.ds(1, HALF, stride=2), :]
                zero = jnp.where(fine_parity == 0, even, odd)
                one = jnp.where(fine_parity == 0, odd, even)
                if put == 0:
                    pa[slot, 0, j + 1, pl.ds(TOP, HALF), :] = zero
                    pa[slot, 1, j + 1, pl.ds(TOP, HALF), :] = one
                else:
                    src_c[slot, 0, j] = zero
                    src_c[slot, 1, j] = one
        return carry

    lax.fori_loop(0, HALF, split, 0)

    def coarse_pairs(s, b, first, q, pairs, first_half):
        cur, nxt = bufs[b], bufs[1 - b]
        which = jnp.where(q == q_start, 0, 1)

        def cell(i):
            if i in (0, PAIRS + 1):
                return near[i // PAIRS]
            return cur[first if first_half else 1 - first, i, rows, :]

        def other(i, at):
            if not first_half:
                return nxt[0, i, at, :]
            if i in (0, PAIRS + 1):
                return halo[i // PAIRS, at, :]
            return cur[1 - first, i, at, :]

        outs = []
        for i in pairs:
            here = other(i, rows)
            if i == 0:
                second = other(1, rows)
            elif i == PAIRS + 1:
                second = other(PAIRS, rows)
            else:
                second = jnp.where(plane_parity == q, other(i - 1, rows), other(i + 1, rows))
            source = rho_h[which, i // PAIRS] if i in (0, PAIRS + 1) else rho_c[q, i - 1]
            outs.append(
                relaxed(
                    cell(i),
                    (
                        here,
                        second,
                        other(i, pl.ds(TOP - 1, N)),
                        other(i, pl.ds(TOP + 1, N)),
                        jnp.where(lane_c == 0, 0.0, pltpu.roll(here, 1, 1)),
                        jnp.where(lane_c == N - 1, 0.0, pltpu.roll(here, N - 1, 1)),
                    ),
                    source,
                )
            )
        for i, out in zip(pairs, outs):
            nxt[0 if first_half else 1, i, rows, :] = out

    def patch_half(slot, center_ref, role_c, other_ref, role_b, out_ref, role_out, q):
        data = pl.ds(TOP, HALF)

        def step(k, carry):
            j0 = k * JB
            b = [other_ref[slot, role_b, j0 + t, data, :] for t in range(JB + 2)]
            across = [pltpu.roll(jnp.where(y_first, b[t + 1], b[t]), FINE, 1) for t in range(JB + 1)]
            outs = []
            for t in range(JB):
                below = other_ref[slot, role_b, j0 + t + 1, pl.ds(TOP - 1, HALF), :]
                above = other_ref[slot, role_b, j0 + t + 1, pl.ds(TOP + 1, HALF), :]
                face = x_face[slot, k * (JB // 2) + t // 2]
                near = b[t + 1]
                outs.append(
                    relaxed(
                        center_ref[slot, role_c, j0 + t + 1, data, :],
                        (
                            near,
                            jnp.where(fine_parity == q, below, above),
                            across[t],
                            across[t + 1],
                            jnp.where(x_first, face, pltpu.roll(near, 1, 1)),
                            jnp.where(x_last, face, pltpu.roll(near, N - 1, 1)),
                        ),
                        src_c[slot, q, j0 + t],
                    )
                )
            for t in range(JB):
                out_ref[slot, role_out, j0 + t + 1, data, :] = outs[t]
            return carry

        lax.fori_loop(0, HALF // JB, step, 0)

    def set_faces(prev, nxt):
        data = pl.ds(TOP, HALF)
        pitch = HALF + 2 * TOP
        w = 4.0 * w_rows[...]
        y_faces, z_faces = [], []
        for slot in range(SLOTS):
            y_faces.append(split_dot(w, ey[slot]))
            oy = jnp.maximum(anchors[1, p * SLOTS + slot], 1)
            z_rows = jnp.concatenate([zplanes[0, pl.ds(oy, WIN), :], zplanes[1, pl.ds(oy, WIN), :]], axis=0)
            z_faces.append(split_dot(z_rows, sx[slot]))
        for slot in range(SLOTS):
            for t in range(WIN):
                at = slot * FINE + t
                low = jnp.broadcast_to(w[:, at : at + 1], (HALF, N))
                high = jnp.broadcast_to(w[:, at + WIN : at + WIN + 1], (HALF, N))
                x_face[slot, t] = jnp.where(x_last, high, low)
        for slot in range(SLOTS):
            for ref, role in ((prev, 0), (prev, 1), (nxt, 0)):
                ref[slot, role, 0, data, :] = y_faces[slot]
                ref[slot, role, HALF + 1, data, :] = y_faces[slot]
                lines = ref.reshape(SLOTS * 2 * (HALF + 2) * pitch, N)
                start = (slot * 2 + role) * (HALF + 2) * pitch
                for t in range(2):
                    low = pl.ds(start + (t + 1) * pitch + TOP - 1, WIN, stride=2 * pitch)
                    high = pl.ds(start + (t + 1) * pitch + TOP + HALF, WIN, stride=2 * pitch)
                    lines[low, :] = z_faces[slot][:WIN]
                    lines[high, :] = z_faces[slot][WIN:]

    patch_bufs = (pa, pb)

    def sweep(s, b, may_end):
        q = order[s]
        before = order[jnp.maximum(s - 1, 0)]
        first = jnp.where(s == 0, q, jnp.where(q == before, 0, 1))
        cur, nxt = bufs[b], bufs[1 - b]

        def unless_last(do):
            if may_end:
                pl.when(s < SWEEPS - 1)(do)
            else:
                do()

        coarse_pairs(s, b, first, q, (2, PAIRS - 1), True)
        for side, ok in sides:
            @pl.when(ok)
            def _(side=side):
                def start_of_all():
                    near_copy(1 - side).wait_recv()
                    pair_copy(s, 1 - side, second_only).wait_recv()
                    near[side] = near_rx[side]

                def later():
                    pair_copy(s, 1 - side, both).wait_recv()
                    mine = plane_parity == (1 - before if side == 0 else before)
                    near[side] = jnp.where(
                        mine, cur[0, side * (PAIRS + 1), rows, :], unfolded(pair_rx[s, side, :FINE, :])
                    )

                if b == 0:
                    pl.when(s == 0)(start_of_all)
                    pl.when(s > 0)(later)
                else:
                    later()
                second = unfolded(pair_rx[s, side, FINE:, :])
                halo[side, rows, :] = jnp.where(
                    plane_parity == (1 - q if side == 0 else q), second, near[side]
                )

                @pl.when(s == b)
                def _():
                    rho_copy(b, 1 - side).wait_recv()
                    rho_h[b, side] = unfolded(rho_rx[b, side])

            @pl.when(jnp.logical_not(ok))
            def _(side=side):
                halo[side, rows, :] = jnp.zeros((N, N), jnp.float32)

        coarse_pairs(s, b, first, q, (1, PAIRS, 0, PAIRS + 1), True)
        for side, ok in sides:
            @pl.when(jnp.logical_not(ok))
            def _(side=side):
                nxt[0, side * (PAIRS + 1), rows, :] = jnp.zeros((N, N), jnp.float32)
        coarse_pairs(s, b, first, 1 - q, (1, PAIRS), False)

        for side, ok in sides:
            @pl.when(ok)
            def _(side=side):
                if b == 0:
                    @pl.when(s == 0)
                    def _():
                        near_copy(side).wait_send()
                        pair_copy(s, side, second_only).wait_send()

                    @pl.when(s > 0)
                    def _():
                        pair_copy(s, side, both).wait_send()
                else:
                    pair_copy(s, side, both).wait_send()

                @pl.when(s == b)
                def _():
                    rho_copy(b, side).wait_send()

        @pl.when(far_to_ok)
        def _():
            far_copy(s).wait_send()

        w_copy(s).wait_send()

        def whole(z):
            role = z % 2
            i = z // 2 + 1
            return jnp.where(plane_parity == q, nxt[role, i, rows, :], nxt[1 - role, i, rows, :])

        def send_outer():
            q_next = order[jnp.minimum(s + 1, SWEEPS - 1)]
            read = jnp.where(q_next == q, 1, 0)
            for side, ok in sides:
                i = PAIRS if side else 1
                last, ahead = (q, 1 - q_next) if side else (1 - q, q_next)
                pair_send[side, :FINE, :] = folded(nxt[1, i, rows, :], last)
                pair_send[side, FINE:, :] = folded(nxt[read, i, rows, :], ahead)

                @pl.when(ok)
                def _(side=side):
                    pair_copy(s + 1, side, both).start()

            full[plane(0), :] = whole(0)
            full[plane(CZ - 1), :] = whole(CZ - 1)
            start_far(s + 1)

        unless_last(send_outer)
        coarse_pairs(s, b, first, 1 - q, (2, PAIRS - 1), False)

        w_copy(s).wait_recv()
        mine, theirs = w_own[...], w_rx[s]
        lower = jnp.where(p == 0, mine, theirs)
        upper = jnp.where(p == 0, theirs, mine)
        for t in range(2):
            w_rows[pl.ds(t, CZ, stride=2), :] = lower
            w_rows[pl.ds(2 * CZ + t, CZ, stride=2), :] = upper

        def send_faces():
            for z in range(1, CZ - 1):
                full[plane(z), :] = whole(z)
            pack_faces()
            w_copy(s + 1).start()

        unless_last(send_faces)
        if may_end:
            @pl.when(s == SWEEPS - 1)
            def _():
                for z in range(CZ):
                    coarse_stage[z] = whole(z)
                pltpu.make_async_copy(coarse_stage, coarse_hbm, out_sem.at[SLOTS]).start()

        @pl.when(far_from_ok)
        def _():
            far_copy(s).wait_recv()

        near_ok = jnp.where(p == 0, has_dn, has_up)
        zplanes[p] = jnp.where(near_ok, 4.0 * near[p], 0.0)
        zplanes[1 - p] = jnp.where(far_from_ok, 4.0 * far_rx[s], 0.0)
        now, new = patch_bufs[b], patch_bufs[1 - b]
        set_faces(now, new)
        def sweep_slot(slot, carry):
            patch_half(slot, now, first, now, 1 - first, new, 0, q)
            patch_half(slot, now, 1 - first, new, 0, new, 1, 1 - q)
            if may_end:
                @pl.when(s == SWEEPS - 1)
                def _():
                    live = slot < owned[p]

                    def join(k, carry):
                        joined = []
                        for t in range(JOIN):
                            j = k * JOIN + t
                            one = 0.25 * new[slot, 0, j + 1, pl.ds(TOP, HALF), :]
                            two = 0.25 * new[slot, 1, j + 1, pl.ds(TOP, HALF), :]
                            for odd in range(2):
                                old = raw_pot[slot, j, pl.ds(odd, HALF, stride=2), :]
                                swept = jnp.where(fine_parity == (q + odd) % 2, one, two)
                                joined.append((j, odd, jnp.where(live, swept, old)))
                        for j, odd, cells in joined:
                            out_stage[slot, j, pl.ds(odd, HALF, stride=2), :] = cells
                        for t in range(JOIN):
                            j = k * JOIN + t
                            pltpu.make_async_copy(
                                out_stage.at[slot, j], patch_hbm.at[slot, :, columns(j)], out_sem.at[slot]
                            ).start()
                        return carry

                    lax.fori_loop(0, HALF // JOIN, join, 0)
            return carry

        lax.fori_loop(0, SLOTS, sweep_slot, 0)

    def two_sweeps(t, carry):
        sweep(2 * t, 0, False)
        sweep(2 * t + 1, 1, True)
        return carry

    lax.fori_loop(0, SWEEPS // 2, two_sweeps, 0)
    pltpu.make_async_copy(coarse_stage, coarse_hbm, out_sem.at[SLOTS]).wait()
    for slot in range(SLOTS):
        pltpu.make_async_copy(out_stage.at[slot], out_stage.at[slot], out_sem.at[slot]).wait()


def on_device(groups, phi, rho, pot, src, anchors, owned, order):
    f32, bf16 = jnp.float32, jnp.bfloat16
    dma = pltpu.SemaphoreType.DMA
    smem = pl.BlockSpec(memory_space=pltpu.SMEM)
    hbm = pl.BlockSpec(memory_space=pltpu.HBM)
    anywhere = pl.BlockSpec(memory_space=pl.ANY)
    return pl.pallas_call(
        functools.partial(kernel, groups),
        out_shape=(pltpu.VMEM(phi.shape, f32), pltpu.VMEM(pot.shape, f32)),
        in_specs=[smem] * 3 + [hbm] * 4,
        out_specs=(anywhere, anywhere),
        scratch_shapes=[
            pltpu.VMEM((CZ * FULL, N), f32),
            pltpu.VMEM((CZ, N, N), f32),
            pltpu.VMEM((SLOTS, HALF, FINE, N), f32),
            pltpu.VMEM((SLOTS, HALF, FINE, N), f32),
            pltpu.VMEM((2, PAIRS + 2, N + 2 * TOP, N), f32),
            pltpu.VMEM((2, PAIRS + 2, N + 2 * TOP, N), f32),
            pltpu.VMEM((2, N + 2 * TOP, N), f32),
            pltpu.VMEM((2, PAIRS, N, N), f32),
            pltpu.VMEM((2, 2, N, N), f32),
            pltpu.VMEM((2, N, N), f32),
            pltpu.VMEM((2, N, N), f32),
            pltpu.VMEM((2, N, N), f32),
            pltpu.VMEM((SWEEPS, 2, N, N), f32),
            pltpu.VMEM((2, 2, FINE, N), f32),
            pltpu.VMEM((2, 2, FINE, N), f32),
            pltpu.VMEM((CZ, N), f32),
            pltpu.VMEM((CZ, N), f32),
            pltpu.VMEM((SWEEPS, CZ, N), f32),
            pltpu.VMEM((SWEEPS, N, N), f32),
            pltpu.VMEM((2, N, N), f32),
            pltpu.VMEM((HALF, N), f32),
            pltpu.VMEM((SLOTS, 2, HALF + 2, HALF + 2 * TOP, N), f32),
            pltpu.VMEM((SLOTS, 2, HALF + 2, HALF + 2 * TOP, N), f32),
            pltpu.VMEM((SLOTS, 2, HALF, HALF, N), f32),
            pltpu.VMEM((SLOTS, WIN, HALF, N), f32),
            pltpu.VMEM((SLOTS, N, N), bf16),
            pltpu.VMEM((SLOTS, N, N), bf16),
            pltpu.VMEM((CZ, N, N), f32),
            pltpu.VMEM((SLOTS, HALF, FINE, N), f32),
            dma((CZ + 3,)),
            dma((SLOTS + 1,)),
            dma((2,)),
            dma((2,)),
            dma((2,)),
            dma((SWEEPS, 2)),
            dma((2, 2)),
            dma((2, 2)),
            dma,
            dma((SWEEPS,)),
            dma,
            dma((SWEEPS,)),
        ],
        compiler_params=pltpu.CompilerParams(
            collective_id=0, has_side_effects=True, vmem_limit_bytes=54000000
        ),
        name="smooth",
    )(anchors.T, owned, order, phi, rho, pot, src)


def solution(mesh):
    in_specs = (
        P(("slab", "patch"), None, None),
        P(("slab", "patch"), None, None),
        P(("slab", "patch"), None, None),
        P(("slab", "patch"), None, None),
        P("slab", None),
        P("slab"),
        P(),
    )
    out_specs = (P(("slab", "patch"), None, None), P(("slab", "patch"), None, None))
    return jax.shard_map(
        functools.partial(on_device, mesh.shape["slab"]),
        mesh=mesh, in_specs=in_specs, out_specs=out_specs, check_vma=False,
    )
```

```python
import functools

import jax
import jax.numpy as jnp
from jax import lax
from jax.experimental import pallas as pl
from jax.experimental.pallas import tpu as pltpu
from jax.sharding import PartitionSpec as P

MESH = pl.DeviceIdType.MESH
SWEEPS = 4
N = 128
CZ = 8
PAIRS = CZ // 2
SLOTS = 2
FINE = 64
HALF = FINE // 2
WIN = 16
TOP = 8
FULL = N + 8
JOIN = 8
JB = 32


def relaxed(center, neighbours, source):
    r_sum = rv_sum = v_sum = None
    for value in neighbours:
        r = pl.reciprocal(1.0 + jnp.abs(value - center), approx=True)
        rv = r * value
        r_sum = r if r_sum is None else r_sum + r
        rv_sum = rv if rv_sum is None else rv_sum + rv
        v_sum = value if v_sum is None else v_sum + value
    return (rv_sum + (v_sum - source)) * pl.reciprocal(6.0 + r_sum, approx=True)


def iota(shape, dim):
    return lax.broadcasted_iota(jnp.int32, shape, dim)


def split_dot(rows, onehot):
    high = rows.astype(jnp.bfloat16)
    low = (rows - high.astype(jnp.float32)).astype(jnp.bfloat16)
    return jnp.dot(high, onehot, preferred_element_type=jnp.float32) + jnp.dot(
        low, onehot, preferred_element_type=jnp.float32
    )


def kernel(
    groups,
    anchors, owned, order, phi_hbm, rho_hbm, pot_hbm, src_hbm,
    coarse_hbm, patch_hbm,
    full, raw_rho, raw_pot, raw_src,
    ca, cb, halo, rho_c, rho_h, near_rx, near, pair_send, pair_rx, rho_send, rho_rx,
    w_own, w_send, w_rx, far_rx, zplanes, w_rows, pa, pb, src_c, x_face, sx, ey, coarse_stage, out_stage,
    in_sem, out_sem, near_ssem, near_rsem, pair_ssem, pair_rsem, rho_ssem, rho_rsem,
    w_ssem, w_rsem, far_ssem, far_rsem,
):
    g = lax.axis_index("slab")
    p = lax.axis_index("patch")
    has_up = jnp.logical_or(g < groups - 1, p == 0)
    has_dn = jnp.logical_or(g > 0, p == 1)
    far_to_ok = jnp.where(p == 0, g > 0, g < groups - 1)
    far_from_ok = jnp.where(p == 0, g < groups - 1, g > 0)
    wrap = lambda v: lax.rem(v + groups, groups)
    up = (wrap(g + p), 1 - p)
    dn = (wrap(g - 1 + p), 1 - p)
    partner = (g, 1 - p)
    far_to = (wrap(g + 2 * p - 1), p)
    far_from = (wrap(g + 1 - 2 * p), p)
    sides = ((0, has_dn), (1, has_up))

    barrier = pltpu.get_barrier_semaphore()
    greeted = ((up, has_up), (dn, has_dn), (far_to, far_to_ok), (far_from, far_from_ok))
    for device, ok in greeted:
        @pl.when(ok)
        def _(device=device):
            pl.semaphore_signal(barrier, inc=1, device_id=device, device_id_type=MESH)

    def plane(z):
        return pl.ds(z * FULL, N)

    loads = [pltpu.make_async_copy(phi_hbm.at[z], full.at[plane(z)], in_sem.at[z]) for z in range(CZ)]
    loads.append(pltpu.make_async_copy(rho_hbm, raw_rho, in_sem.at[CZ]))
    for load in loads:
        load.start()

    def columns(j):
        return pl.ds(pl.multiple_of(j * N, N), N)

    def fetch(j, carry):
        for slot in range(SLOTS):
            pltpu.make_async_copy(
                pot_hbm.at[slot, :, columns(j)], raw_pot.at[slot, j], in_sem.at[CZ + 1]
            ).start()
            pltpu.make_async_copy(
                src_hbm.at[slot, :, columns(j)], raw_src.at[slot, j], in_sem.at[CZ + 2]
            ).start()
        return carry

    rows = pl.ds(TOP, N)
    bufs = (ca, cb)

    def near_copy(side):
        return pltpu.make_async_remote_copy(
            src_ref=full.at[plane(side * (CZ - 1))], dst_ref=near_rx.at[1 - side],
            send_sem=near_ssem.at[side], recv_sem=near_rsem.at[1 - side],
            device_id=(dn, up)[side], device_id_type=MESH,
        )

    def pair_copy(s, side, at):
        return pltpu.make_async_remote_copy(
            src_ref=pair_send.at[side, at], dst_ref=pair_rx.at[s, 1 - side, at],
            send_sem=pair_ssem.at[side], recv_sem=pair_rsem.at[s, 1 - side],
            device_id=(dn, up)[side], device_id_type=MESH,
        )

    def rho_copy(which, side):
        return pltpu.make_async_remote_copy(
            src_ref=rho_send.at[which, side], dst_ref=rho_rx.at[which, 1 - side],
            send_sem=rho_ssem.at[which, side], recv_sem=rho_rsem.at[which, 1 - side],
            device_id=(dn, up)[side], device_id_type=MESH,
        )

    def w_copy(s):
        return pltpu.make_async_remote_copy(
            src_ref=w_send, dst_ref=w_rx.at[s], send_sem=w_ssem, recv_sem=w_rsem.at[s],
            device_id=partner, device_id_type=MESH,
        )

    def far_copy(s):
        return pltpu.make_async_remote_copy(
            src_ref=full.at[pl.ds(p * ((CZ - 1) * FULL), N)], dst_ref=far_rx.at[s],
            send_sem=far_ssem, recv_sem=far_rsem.at[s],
            device_id=far_to, device_id_type=MESH,
        )

    plane_parity = (iota((N, N), 0) + iota((N, N), 1)) % 2
    half_parity = (iota((FINE, N), 0) + iota((FINE, N), 1)) % 2
    lane_c = iota((N, N), 1)
    lane_p = iota((HALF, N), 1)
    fine_parity = (lane_p // FINE + lane_p) % 2
    x_first = lane_p % FINE == 0
    x_last = lane_p % FINE == FINE - 1
    y_first = lane_p < FINE

    def folded(cells, parity):
        return jnp.where(half_parity == parity, cells[:FINE], pltpu.roll(cells[FINE:], 1, 1))

    def unfolded(cells):
        return jnp.concatenate([cells, pltpu.roll(cells, N - 1, 1)], axis=0)

    for ref, lead in ((ca, 2), (cb, 2), (halo, 0)):
        for role in range(max(lead, 1)):
            for i in range(PAIRS + 2 if lead else 2):
                where = (role, i) if lead else (i,)
                ref[(*where, slice(0, TOP), slice(None))] = jnp.zeros((TOP, N), jnp.float32)
                ref[(*where, slice(TOP + N, None), slice(None))] = jnp.zeros((TOP, N), jnp.float32)

    def pack_faces():
        lane = iota((CZ, N), 1)
        for whose, dst in ((1 - p, w_send), (p, w_own)):
            packed = jnp.zeros((CZ, N), jnp.float32)
            for k in range(SLOTS):
                ox = anchors[0, whose * SLOTS + k]
                oy = jnp.maximum(anchors[1, whose * SLOTS + k], 1)
                base = k * FINE
                for t in range(WIN):
                    line = full[pl.ds(oy + t, CZ, stride=FULL), :]
                    low = pltpu.roll(line, lax.rem(base + t - (ox - 1) + 2 * N, N), 1)
                    high = pltpu.roll(line, lax.rem(base + WIN + t - (ox + WIN) + 2 * N, N), 1)
                    packed = jnp.where(lane == base + t, low, packed)
                    packed = jnp.where(lane == base + WIN + t, high, packed)
                for kind, row in ((2, oy - 1), (3, oy + WIN)):
                    line = full[pl.ds(row, CZ, stride=FULL), :]
                    line = pltpu.roll(line, lax.rem(base + kind * WIN - ox + 2 * N, N), 1)
                    inside = jnp.logical_and(lane >= base + kind * WIN, lane < base + (kind + 1) * WIN)
                    packed = jnp.where(inside, line, packed)
            dst[...] = packed

    q_start = order[0]
    for z in range(CZ):
        loads[z].wait()
    for i in range(PAIRS):
        even, odd = full[plane(2 * i), :], full[plane(2 * i + 1), :]
        ca[0, i + 1, rows, :] = jnp.where(plane_parity == 0, even, odd)
        ca[1, i + 1, rows, :] = jnp.where(plane_parity == 0, odd, even)
    pair_send[0, FINE:, :] = folded(full[plane(1), :], q_start)
    pair_send[1, FINE:, :] = folded(full[plane(CZ - 2), :], 1 - q_start)
    loads[CZ].wait()
    for which in range(2):
        rho_send[which, 0] = folded(raw_rho[0], (q_start + which) % 2)
        rho_send[which, 1] = folded(raw_rho[CZ - 1], (q_start + which + 1) % 2)

    pl.semaphore_wait(barrier, sum(ok.astype(jnp.int32) for _, ok in greeted))

    def start_rho(which):
        for side, ok in sides:
            @pl.when(ok)
            def _(side=side):
                rho_copy(which, side).start()

    def start_far(s):
        @pl.when(far_to_ok)
        def _():
            far_copy(s).start()

    both, second_only = pl.ds(0, N), pl.ds(FINE, FINE)
    for side, ok in sides:
        @pl.when(ok)
        def _(side=side):
            near_copy(side).start()
    for side, ok in sides:
        @pl.when(ok)
        def _(side=side):
            pair_copy(0, side, second_only).start()
    start_rho(0)
    start_far(0)
    start_rho(1)
    pack_faces()
    w_copy(0).start()
    lax.fori_loop(0, HALF, fetch, 0)

    for i in range(PAIRS):
        even, odd = raw_rho[2 * i], raw_rho[2 * i + 1]
        rho_c[0, i] = jnp.where(plane_parity == 0, even, odd)
        rho_c[1, i] = jnp.where(plane_parity == 0, odd, even)

    for slot in range(SLOTS):
        ox = anchors[0, p * SLOTS + slot]
        row, lane = iota((N, N), 0), lane_c
        sx[slot] = (row == ox + (lane % FINE) // 4).astype(jnp.float32).astype(jnp.bfloat16)
        wanted = slot * FINE + jnp.where(lane < FINE, 3 * WIN, 2 * WIN) + (lane % FINE) // 4
        ey[slot] = (row == wanted).astype(jnp.float32).astype(jnp.bfloat16)
    pltpu.make_async_copy(raw_pot, raw_pot, in_sem.at[CZ + 1]).wait()
    pltpu.make_async_copy(raw_src, raw_src, in_sem.at[CZ + 2]).wait()

    def split(j, carry):
        for slot in range(SLOTS):
            for raw, scale, put in ((raw_pot, 4.0, 0), (raw_src, 0.25, 1)):
                even = scale * raw[slot, j, pl.ds(0, HALF, stride=2), :]
                odd = scale * raw[slot, j, pl.ds(1, HALF, stride=2), :]
                zero = jnp.where(fine_parity == 0, even, odd)
                one = jnp.where(fine_parity == 0, odd, even)
                if put == 0:
                    pa[slot, 0, j + 1, pl.ds(TOP, HALF), :] = zero
                    pa[slot, 1, j + 1, pl.ds(TOP, HALF), :] = one
                else:
                    src_c[slot, 0, j] = zero
                    src_c[slot, 1, j] = one
        return carry

    lax.fori_loop(0, HALF, split, 0)

    def coarse_pairs(s, b, first, q, pairs, first_half):
        cur, nxt = bufs[b], bufs[1 - b]
        which = jnp.where(q == q_start, 0, 1)

        def cell(i):
            if i in (0, PAIRS + 1):
                return near[i // PAIRS]
            return cur[first if first_half else 1 - first, i, rows, :]

        def other(i, at):
            if not first_half:
                return nxt[0, i, at, :]
            if i in (0, PAIRS + 1):
                return halo[i // PAIRS, at, :]
            return cur[1 - first, i, at, :]

        outs = []
        for i in pairs:
            here = other(i, rows)
            if i == 0:
                second = other(1, rows)
            elif i == PAIRS + 1:
                second = other(PAIRS, rows)
            else:
                second = jnp.where(plane_parity == q, other(i - 1, rows), other(i + 1, rows))
            source = rho_h[which, i // PAIRS] if i in (0, PAIRS + 1) else rho_c[q, i - 1]
            outs.append(
                relaxed(
                    cell(i),
                    (
                        here,
                        second,
                        other(i, pl.ds(TOP - 1, N)),
                        other(i, pl.ds(TOP + 1, N)),
                        jnp.where(lane_c == 0, 0.0, pltpu.roll(here, 1, 1)),
                        jnp.where(lane_c == N - 1, 0.0, pltpu.roll(here, N - 1, 1)),
                    ),
                    source,
                )
            )
        for i, out in zip(pairs, outs):
            nxt[0 if first_half else 1, i, rows, :] = out

    def patch_half(slot, center_ref, role_c, other_ref, role_b, out_ref, role_out, q):
        data = pl.ds(TOP, HALF)

        def step(k, carry):
            j0 = k * JB
            b = [other_ref[slot, role_b, j0 + t, data, :] for t in range(JB + 2)]
            across = [pltpu.roll(jnp.where(y_first, b[t + 1], b[t]), FINE, 1) for t in range(JB + 1)]
            outs = []
            for t in range(JB):
                below = other_ref[slot, role_b, j0 + t + 1, pl.ds(TOP - 1, HALF), :]
                above = other_ref[slot, role_b, j0 + t + 1, pl.ds(TOP + 1, HALF), :]
                face = x_face[slot, k * (JB // 2) + t // 2]
                near = b[t + 1]
                outs.append(
                    relaxed(
                        center_ref[slot, role_c, j0 + t + 1, data, :],
                        (
                            near,
                            jnp.where(fine_parity == q, below, above),
                            across[t],
                            across[t + 1],
                            jnp.where(x_first, face, pltpu.roll(near, 1, 1)),
                            jnp.where(x_last, face, pltpu.roll(near, N - 1, 1)),
                        ),
                        src_c[slot, q, j0 + t],
                    )
                )
            for t in range(JB):
                out_ref[slot, role_out, j0 + t + 1, data, :] = outs[t]
            return carry

        lax.fori_loop(0, HALF // JB, step, 0)

    def set_faces(prev, nxt):
        data = pl.ds(TOP, HALF)
        pitch = HALF + 2 * TOP
        w = 4.0 * w_rows[...]
        y_faces, z_faces = [], []
        for slot in range(SLOTS):
            y_faces.append(split_dot(w, ey[slot]))
            oy = jnp.maximum(anchors[1, p * SLOTS + slot], 1)
            z_rows = jnp.concatenate([zplanes[0, pl.ds(oy, WIN), :], zplanes[1, pl.ds(oy, WIN), :]], axis=0)
            z_faces.append(split_dot(z_rows, sx[slot]))
        for slot in range(SLOTS):
            for t in range(WIN):
                at = slot * FINE + t
                low = jnp.broadcast_to(w[:, at : at + 1], (HALF, N))
                high = jnp.broadcast_to(w[:, at + WIN : at + WIN + 1], (HALF, N))
                x_face[slot, t] = jnp.where(x_last, high, low)
        for slot in range(SLOTS):
            for ref, role in ((prev, 0), (prev, 1), (nxt, 0)):
                ref[slot, role, 0, data, :] = y_faces[slot]
                ref[slot, role, HALF + 1, data, :] = y_faces[slot]
                lines = ref.reshape(SLOTS * 2 * (HALF + 2) * pitch, N)
                start = (slot * 2 + role) * (HALF + 2) * pitch
                for t in range(2):
                    low = pl.ds(start + (t + 1) * pitch + TOP - 1, WIN, stride=2 * pitch)
                    high = pl.ds(start + (t + 1) * pitch + TOP + HALF, WIN, stride=2 * pitch)
                    lines[low, :] = z_faces[slot][:WIN]
                    lines[high, :] = z_faces[slot][WIN:]

    patch_bufs = (pa, pb)

    def sweep(s, b, may_end):
        q = order[s]
        before = order[jnp.maximum(s - 1, 0)]
        first = jnp.where(s == 0, q, jnp.where(q == before, 0, 1))
        cur, nxt = bufs[b], bufs[1 - b]

        def unless_last(do):
            if may_end:
                pl.when(s < SWEEPS - 1)(do)
            else:
                do()

        coarse_pairs(s, b, first, q, (2, PAIRS - 1), True)
        for side, ok in sides:
            @pl.when(ok)
            def _(side=side):
                def start_of_all():
                    near_copy(1 - side).wait_recv()
                    pair_copy(s, 1 - side, second_only).wait_recv()
                    near[side] = near_rx[side]

                def later():
                    pair_copy(s, 1 - side, both).wait_recv()
                    mine = plane_parity == (1 - before if side == 0 else before)
                    near[side] = jnp.where(
                        mine, cur[0, side * (PAIRS + 1), rows, :], unfolded(pair_rx[s, side, :FINE, :])
                    )

                if b == 0:
                    pl.when(s == 0)(start_of_all)
                    pl.when(s > 0)(later)
                else:
                    later()
                second = unfolded(pair_rx[s, side, FINE:, :])
                halo[side, rows, :] = jnp.where(
                    plane_parity == (1 - q if side == 0 else q), second, near[side]
                )

                @pl.when(s == b)
                def _():
                    rho_copy(b, 1 - side).wait_recv()
                    rho_h[b, side] = unfolded(rho_rx[b, side])

            @pl.when(jnp.logical_not(ok))
            def _(side=side):
                halo[side, rows, :] = jnp.zeros((N, N), jnp.float32)

        coarse_pairs(s, b, first, q, (1, PAIRS, 0, PAIRS + 1), True)
        for side, ok in sides:
            @pl.when(jnp.logical_not(ok))
            def _(side=side):
                nxt[0, side * (PAIRS + 1), rows, :] = jnp.zeros((N, N), jnp.float32)
        coarse_pairs(s, b, first, 1 - q, (1, PAIRS), False)

        for side, ok in sides:
            @pl.when(ok)
            def _(side=side):
                if b == 0:
                    @pl.when(s == 0)
                    def _():
                        near_copy(side).wait_send()
                        pair_copy(s, side, second_only).wait_send()

                    @pl.when(s > 0)
                    def _():
                        pair_copy(s, side, both).wait_send()
                else:
                    pair_copy(s, side, both).wait_send()

                @pl.when(s == b)
                def _():
                    rho_copy(b, side).wait_send()

        @pl.when(far_to_ok)
        def _():
            far_copy(s).wait_send()

        w_copy(s).wait_send()

        def whole(z):
            role = z % 2
            i = z // 2 + 1
            return jnp.where(plane_parity == q, nxt[role, i, rows, :], nxt[1 - role, i, rows, :])

        def send_outer():
            q_next = order[jnp.minimum(s + 1, SWEEPS - 1)]
            read = jnp.where(q_next == q, 1, 0)
            for side, ok in sides:
                i = PAIRS if side else 1
                last, ahead = (q, 1 - q_next) if side else (1 - q, q_next)
                pair_send[side, :FINE, :] = folded(nxt[1, i, rows, :], last)
                pair_send[side, FINE:, :] = folded(nxt[read, i, rows, :], ahead)

                @pl.when(ok)
                def _(side=side):
                    pair_copy(s + 1, side, both).start()

            full[plane(0), :] = whole(0)
            full[plane(CZ - 1), :] = whole(CZ - 1)
            start_far(s + 1)

        unless_last(send_outer)
        coarse_pairs(s, b, first, 1 - q, (2, PAIRS - 1), False)

        w_copy(s).wait_recv()
        mine, theirs = w_own[...], w_rx[s]
        lower = jnp.where(p == 0, mine, theirs)
        upper = jnp.where(p == 0, theirs, mine)
        for t in range(2):
            w_rows[pl.ds(t, CZ, stride=2), :] = lower
            w_rows[pl.ds(2 * CZ + t, CZ, stride=2), :] = upper

        def send_faces():
            for z in range(1, CZ - 1):
                full[plane(z), :] = whole(z)
            pack_faces()
            w_copy(s + 1).start()

        unless_last(send_faces)
        if may_end:
            @pl.when(s == SWEEPS - 1)
            def _():
                for z in range(CZ):
                    coarse_stage[z] = whole(z)
                pltpu.make_async_copy(coarse_stage, coarse_hbm, out_sem.at[SLOTS]).start()

        @pl.when(far_from_ok)
        def _():
            far_copy(s).wait_recv()

        near_ok = jnp.where(p == 0, has_dn, has_up)
        zplanes[p] = jnp.where(near_ok, 4.0 * near[p], 0.0)
        zplanes[1 - p] = jnp.where(far_from_ok, 4.0 * far_rx[s], 0.0)
        now, new = patch_bufs[b], patch_bufs[1 - b]
        set_faces(now, new)
        def sweep_slot(slot, carry):
            patch_half(slot, now, first, now, 1 - first, new, 0, q)
            patch_half(slot, now, 1 - first, new, 0, new, 1, 1 - q)
            if may_end:
                @pl.when(s == SWEEPS - 1)
                def _():
                    live = slot < owned[p]

                    def join(k, carry):
                        joined = []
                        for t in range(JOIN):
                            j = k * JOIN + t
                            one = 0.25 * new[slot, 0, j + 1, pl.ds(TOP, HALF), :]
                            two = 0.25 * new[slot, 1, j + 1, pl.ds(TOP, HALF), :]
                            for odd in range(2):
                                old = raw_pot[slot, j, pl.ds(odd, HALF, stride=2), :]
                                swept = jnp.where(fine_parity == (q + odd) % 2, one, two)
                                joined.append((j, odd, jnp.where(live, swept, old)))
                        for j, odd, cells in joined:
                            out_stage[slot, j, pl.ds(odd, HALF, stride=2), :] = cells
                        for t in range(JOIN):
                            j = k * JOIN + t
                            pltpu.make_async_copy(
                                out_stage.at[slot, j], patch_hbm.at[slot, :, columns(j)], out_sem.at[slot]
                            ).start()
                        return carry

                    lax.fori_loop(0, HALF // JOIN, join, 0)
            return carry

        lax.fori_loop(0, SLOTS, sweep_slot, 0)

    def two_sweeps(t, carry):
        sweep(2 * t, 0, False)
        sweep(2 * t + 1, 1, True)
        return carry

    lax.fori_loop(0, SWEEPS // 2, two_sweeps, 0)
    pltpu.make_async_copy(coarse_stage, coarse_hbm, out_sem.at[SLOTS]).wait()
    for slot in range(SLOTS):
        pltpu.make_async_copy(out_stage.at[slot], out_stage.at[slot], out_sem.at[slot]).wait()


def on_device(groups, phi, rho, pot, src, anchors, owned, order):
    f32, bf16 = jnp.float32, jnp.bfloat16
    dma = pltpu.SemaphoreType.DMA
    smem = pl.BlockSpec(memory_space=pltpu.SMEM)
    hbm = pl.BlockSpec(memory_space=pltpu.HBM)
    anywhere = pl.BlockSpec(memory_space=pl.ANY)
    return pl.pallas_call(
        functools.partial(kernel, groups),
        out_shape=(pltpu.VMEM(phi.shape, f32), pltpu.VMEM(pot.shape, f32)),
        in_specs=[smem] * 3 + [hbm] * 4,
        out_specs=(anywhere, anywhere),
        scratch_shapes=[
            pltpu.VMEM((CZ * FULL, N), f32),
            pltpu.VMEM((CZ, N, N), f32),
            pltpu.VMEM((SLOTS, HALF, FINE, N), f32),
            pltpu.VMEM((SLOTS, HALF, FINE, N), f32),
            pltpu.VMEM((2, PAIRS + 2, N + 2 * TOP, N), f32),
            pltpu.VMEM((2, PAIRS + 2, N + 2 * TOP, N), f32),
            pltpu.VMEM((2, N + 2 * TOP, N), f32),
            pltpu.VMEM((2, PAIRS, N, N), f32),
            pltpu.VMEM((2, 2, N, N), f32),
            pltpu.VMEM((2, N, N), f32),
            pltpu.VMEM((2, N, N), f32),
            pltpu.VMEM((2, N, N), f32),
            pltpu.VMEM((SWEEPS, 2, N, N), f32),
            pltpu.VMEM((2, 2, FINE, N), f32),
            pltpu.VMEM((2, 2, FINE, N), f32),
            pltpu.VMEM((CZ, N), f32),
            pltpu.VMEM((CZ, N), f32),
            pltpu.VMEM((SWEEPS, CZ, N), f32),
            pltpu.VMEM((SWEEPS, N, N), f32),
            pltpu.VMEM((2, N, N), f32),
            pltpu.VMEM((HALF, N), f32),
            pltpu.VMEM((SLOTS, 2, HALF + 2, HALF + 2 * TOP, N), f32),
            pltpu.VMEM((SLOTS, 2, HALF + 2, HALF + 2 * TOP, N), f32),
            pltpu.VMEM((SLOTS, 2, HALF, HALF, N), f32),
            pltpu.VMEM((SLOTS, WIN, HALF, N), f32),
            pltpu.VMEM((SLOTS, N, N), bf16),
            pltpu.VMEM((SLOTS, N, N), bf16),
            pltpu.VMEM((CZ, N, N), f32),
            pltpu.VMEM((SLOTS, HALF, FINE, N), f32),
            dma((CZ + 3,)),
            dma((SLOTS + 1,)),
            dma((2,)),
            dma((2,)),
            dma((2,)),
            dma((SWEEPS, 2)),
            dma((2, 2)),
            dma((2, 2)),
            dma,
            dma((SWEEPS,)),
            dma,
            dma((SWEEPS,)),
        ],
        compiler_params=pltpu.CompilerParams(
            collective_id=0, has_side_effects=True, vmem_limit_bytes=54000000
        ),
        name="smooth",
    )(anchors.T, owned, order, phi, rho, pot, src)


def solution(mesh):
    in_specs = (
        P(("slab", "patch"), None, None),
        P(("slab", "patch"), None, None),
        P(("slab", "patch"), None, None),
        P(("slab", "patch"), None, None),
        P("slab", None),
        P("slab"),
        P(),
    )
    out_specs = (P(("slab", "patch"), None, None), P(("slab", "patch"), None, None))
    return jax.shard_map(
        functools.partial(on_device, mesh.shape["slab"]),
        mesh=mesh, in_specs=in_specs, out_specs=out_specs, check_vma=False,
    )
```
